32 devices in a mesh: bead: 8 (over y, x, core), dom: 4 (over z).
Axes of the slice: x: 2, y: 2, z: 4, core: 2. Of those that a mesh axis runs over, the one named last changes fastest.
Arguments:
- positions: float32 [8, 3, 4096], P('bead', None, 'dom')
- momenta: float32 [8, 3, 4096], P('bead', None, 'dom'), may hold values from -6 to 6
- features: float32 [64, 4096], P(None, 'dom'), may hold values from -6 to 6
- masses: float32 [4096], P('dom'), may hold values from 1 to 16
- radial_width: float32 [4], replicated, may hold values from 1 to 4
- msg_weight: bfloat16 [4, 64, 64], replicated, may hold values from -0.75 to 0.75
- update_weight: bfloat16 [64, 64], replicated, may hold values from -0.75 to 0.75
- mix_weight: bfloat16 [64, 64], replicated, may hold values from -0.75 to 0.75
- out_weight: bfloat16 [64], replicated, may hold values from -4 to 4
- counts: int32 [32], P('dom'), may hold values from 0 to 128, as said below
- pairs: int32 [2, 480], P(None, 'dom'), may hold values from 0 to 23, as said below
- npairs: int32 [4], P('dom'), may hold values from 0 to 120
- leaving: int32 [2, 256], P(None, 'dom'), may hold values from -1 to 1023, as said below
Outputs:
- forces: float32 [8, 3, 4096], P('bead', None, 'dom')
- positions_new: float32 [8, 3, 4096], P('bead', None, 'dom')
- momenta_new: float32 [8, 3, 4096], P('bead', None, 'dom')
- arrivals: float32 [8, 6, 512], P('bead', None, 'dom')
The draws below stay inside these ranges and needn't reach their ends.
Inputs may be any that keep to these rules, and one draw needn't show every extreme that they name: Each block holds atoms in its first counts slots; the first block of every domain is full, and at least one domain has all blocks holding atoms. `pairs`: the first npairs[d] columns of domain d name a local block (row 0, 0 to 7) and an extended block (row 1) numbered over the blocks of d - 1, d, d + 1; both hold atoms and no pair appears twice; later columns are zero. Row 0 names slots of atoms leaving through the lower face, row 1 through the upper face; only occupied slots, no slot twice in a domain, both rows of a domain equally long, -1 after the used entries.
All inputs are finite; a program needn't handle non-finite values.
Results may differ from the reference program's by a relative error of at most 0.0048.
Values sent between devices are 32-bit elements; how exact they have to be, the bound alone decides.
No kernel may reach another device: no remote copies, remote signals or barrier semaphores. Data moves between devices by JAX's collectives and lax.ppermute only.
A program may use at most 64 MiB of HBM per device.

```python
import math
from functools import partial
import jax
import jax.numpy as jnp
import numpy as np
from jax import lax

F = 64
RAD = 4
BLK = 128
GX = 4
GY = 2
MIG = 64
GROUP = 8
CELLS = 8
ATOMS_DEV = 1024
DOMAINS = 4
BEADS = 8
ATOMS = 4096
PMAX = 120


def liquid_domains():
    run_length = max(3, DOMAINS // 4)
    first_liquid = DOMAINS // 2 - run_length // 2
    domain_index = jnp.arange(DOMAINS)
    return (domain_index >= first_liquid) & (domain_index < first_liquid + run_length)


def block_counts(key):
    base_key = jax.random.fold_in(key, 101)
    dense_key, alive_key, sparse_key = jax.random.split(base_key, 3)
    dense_counts = jax.random.randint(dense_key, (DOMAINS, CELLS), 3 * BLK // 4, BLK + 1)
    alive_blocks = (jax.random.randint(alive_key, (DOMAINS, CELLS), 0, 4) == 0).astype(jnp.int32)
    sparse_counts = jax.random.randint(sparse_key, (DOMAINS, CELLS), 1, BLK // 8 + 1) * alive_blocks
    chosen = jnp.where(liquid_domains()[:, None], dense_counts, sparse_counts)
    chosen = chosen.at[:, 0].set(BLK)
    return chosen.astype(jnp.int32)


def candidate_pairs():
    local_list = []
    extended_list = []
    for across in range(GX):
        for sideways in range(GY):
            for layer_step in (-1, 0, 1):
                for across_step in (-1, 0, 1):
                    for sideways_step in (-1, 0, 1):
                        target_across = across + across_step
                        target_sideways = sideways + sideways_step
                        if 0 <= target_across < GX and 0 <= target_sideways < GY:
                            local_list.append(across * GY + sideways)
                            extended_list.append((layer_step + 1) * CELLS + target_across * GY + target_sideways)
    return (np.array(local_list, np.int32), np.array(extended_list, np.int32))


def pair_tables(key):
    counts_grid = block_counts(key)
    local_blocks, extended_blocks = candidate_pairs()
    live_blocks = (counts_grid > 0).astype(jnp.int32)
    live_extended = jnp.concatenate([jnp.roll(live_blocks, 1, axis=0), live_blocks, jnp.roll(live_blocks, -1, axis=0)], axis=1)
    usable = live_blocks[:, local_blocks] * live_extended[:, extended_blocks]
    order_keys = jax.random.split(jax.random.fold_in(key, 202), DOMAINS)
    shuffles = jax.vmap(lambda order_key: jax.random.permutation(order_key, PMAX))(order_keys)
    ordering = jnp.argsort((1 - usable) * PMAX + shuffles, axis=1)
    sorted_usable = jnp.take_along_axis(usable, ordering, axis=1)
    local_sorted = jnp.take(jnp.asarray(local_blocks), ordering) * sorted_usable
    extended_sorted = jnp.take(jnp.asarray(extended_blocks), ordering) * sorted_usable
    return (local_sorted, extended_sorted, jnp.sum(usable, axis=1))


def draw_counts(key, part):
    return block_counts(key).reshape(DOMAINS * CELLS)


def draw_pairs(key, part):
    local_sorted, extended_sorted, totals = pair_tables(key)
    return jnp.stack([local_sorted.reshape(-1), extended_sorted.reshape(-1)], axis=0).astype(jnp.int32)


def draw_npairs(key, part):
    return pair_tables(key)[2].astype(jnp.int32)


def draw_leaving(key, part):
    counts_grid = block_counts(key)
    slot_index = jnp.arange(BLK)
    live_atoms = (slot_index[None, None, :] < counts_grid[:, :, None]).astype(jnp.int32).reshape(DOMAINS, ATOMS_DEV)
    shuffle_keys = jax.random.split(jax.random.fold_in(key, 303), DOMAINS)
    shuffles = jax.vmap(lambda shuffle_key: jax.random.permutation(shuffle_key, ATOMS_DEV))(shuffle_keys)
    ordering = jnp.argsort((1 - live_atoms) * ATOMS_DEV + shuffles, axis=1)
    movers = jnp.minimum(MIG, jnp.sum(live_atoms, axis=1) // 2)
    places = jnp.arange(MIG)
    lower_face = jnp.where(places[None, :] < movers[:, None], ordering[:, :MIG], -1)
    upper_pick = jnp.take_along_axis(ordering, movers[:, None] + places[None, :], axis=1)
    upper_face = jnp.where(places[None, :] < movers[:, None], upper_pick, -1)
    return jnp.stack([lower_face.reshape(-1), upper_face.reshape(-1)], axis=0).astype(jnp.int32)


def draw_positions(key, part):
    centre_key, bead_key = jax.random.split(jax.random.fold_in(key, 404))
    block_index = jnp.arange(ATOMS) // BLK % CELLS
    across = (block_index // GY).astype(jnp.float32)
    sideways = (block_index % GY).astype(jnp.float32)
    centres = jnp.stack([(across + 0.5) * 10.0, (sideways + 0.5) * 10.0, jnp.full((ATOMS,), 5.0, jnp.float32)], axis=0)
    offsets = jax.random.uniform(centre_key, (3, ATOMS), minval=-5.0, maxval=5.0)
    bead_shift = 0.2 * jax.random.normal(bead_key, (BEADS, 3, ATOMS))
    return ((centres + offsets)[None] + bead_shift).astype(jnp.float32)


def shard_levels(key, extent, pieces, least, top_value):
    def one(dim, shards_of):
        steps = jax.random.uniform(jax.random.fold_in(jax.random.fold_in(key, 6), dim), (shards_of,), jnp.float32, least / len(pieces), top_value / len(pieces))
        return jnp.repeat(jnp.exp(steps), extent[dim] // shards_of).reshape((-1,) + (1,) * (len(extent) - dim - 1))

    loudness = one(*pieces[0])
    for cut in pieces[1:]:
        loudness = loudness * one(*cut)
    return loudness


def gaussian(own_key, extent, deviation, reach, shards=(), kind=jnp.bfloat16):
    drawn = deviation * jax.random.normal(own_key, extent, jnp.float32)
    if shards:
        drawn = drawn * shard_levels(own_key, extent, shards, -0.22, 0.18)
    return jnp.clip(drawn, -reach, reach).astype(kind)


def setup_inputs(seed: int = 0) -> dict:
    streams_of = jax.random.split(jax.random.key(seed), 14)
    positions = draw_positions(jax.random.fold_in(streams_of[13], 71), 0)
    momenta = gaussian(streams_of[1], (BEADS, 3, ATOMS), 1.0, 6.0, ((0, 8), (2, 4)), jnp.float32)
    features = gaussian(streams_of[2], (F, ATOMS), 1.0, 6.0, ((1, 4),), jnp.float32)
    masses = jnp.clip(jnp.exp(math.log(16.0) - 2.7725887 * jax.random.uniform(streams_of[3], (ATOMS,), jnp.float32) ** shard_levels(streams_of[3], (ATOMS,), ((0, 4),), -0.2, 0.2)), 1.0, 16.0)
    radial_width = jnp.clip(jax.random.uniform(streams_of[4], (RAD,), jnp.float32, 1.0, 4.0), 1.0, 4.0)
    msg_weight = gaussian(streams_of[5], (RAD, F, F), F ** -0.5, 0.75)
    update_weight = gaussian(streams_of[6], (F, F), F ** -0.5, 0.75)
    mix_weight = gaussian(streams_of[7], (F, F), F ** -0.5, 0.75)
    out_weight = gaussian(streams_of[8], (F,), 1.0, 4.0)
    counts = draw_counts(jax.random.fold_in(streams_of[13], 71), 0)
    pairs = draw_pairs(jax.random.fold_in(streams_of[13], 71), 0)
    npairs = draw_npairs(jax.random.fold_in(streams_of[13], 71), 0)
    leaving = draw_leaving(jax.random.fold_in(streams_of[13], 71), 0)
    return {"positions": positions, "momenta": momenta, "features": features, "masses": masses, "radial_width": radial_width, "msg_weight": msg_weight, "update_weight": update_weight, "mix_weight": mix_weight, "out_weight": out_weight, "counts": counts, "pairs": pairs, "npairs": npairs, "leaving": leaving}


CUTOFF_SQUARE = 36.0
CELL_SIDE = 10.0
MESSAGE_SCALE = 0.25
SPRING_RATE = 0.2


def radial_terms(squared, inverse_width):
    inside = squared < CUTOFF_SQUARE
    remain = 1.0 - squared / CUTOFF_SQUARE
    cutoff = jnp.where(inside, remain * remain, 0.0)[:, None]
    cutoff_slope = jnp.where(inside, -2.0 * remain / CUTOFF_SQUARE, 0.0)[:, None]
    widths = inverse_width[None, :, None, None]
    decays = jnp.exp(-squared[:, None] * widths)
    values = decays * cutoff
    slopes = decays * (cutoff_slope - cutoff * widths)
    return values, slopes


def pair_geometry(coords, row_index, column_index, same_block, weight):
    row_points = jnp.take(coords, row_index, axis=0, mode="clip")
    column_points = jnp.take(coords, column_index, axis=0, mode="clip")
    separation = row_points[:, :, :, None] - column_points[:, :, None, :]
    squared = jnp.sum(separation * separation, axis=1)
    block_size = row_points.shape[2]
    identity = (lax.broadcasted_iota(jnp.int32, (block_size, block_size), 0) == lax.broadcasted_iota(jnp.int32, (block_size, block_size), 1)).astype(jnp.float32)
    keep_mask = weight[:, None, None] * (1.0 - same_block[:, None, None] * identity[None])
    return separation, squared, keep_mask


def clamp_index(index, limit):
    return jnp.clip(index, 0, limit - 1)


def message_group(coords, tables, inverse_width, summed, row_index, column_index, out_index, same_block, weight):
    row_index = clamp_index(row_index, coords.shape[0])
    column_index = clamp_index(column_index, coords.shape[0])
    separation, squared, keep_mask = pair_geometry(coords, row_index, column_index, same_block, weight)
    values, slopes = radial_terms(squared, inverse_width)
    amplitude = (values * keep_mask[:, None]).astype(jnp.bfloat16)
    gathered = jnp.take(tables, column_index, axis=0, mode="clip")
    contrib = jnp.einsum("gfke,gkie->gfi", gathered.astype(jnp.float32), amplitude.astype(jnp.float32))
    return summed.at[out_index].add(contrib)


def force_group(coords, tables, downstream, inverse_width, summed, row_index, column_index, out_index, same_block, weight):
    row_index = clamp_index(row_index, coords.shape[0])
    column_index = clamp_index(column_index, coords.shape[0])
    separation, squared, keep_mask = pair_geometry(coords, row_index, column_index, same_block, weight)
    values, slopes = radial_terms(squared, inverse_width)
    gathered = jnp.take(tables, column_index, axis=0, mode="clip")
    incoming = jnp.take(downstream, out_index, axis=0, mode="clip")
    pair_grad = jnp.einsum("gfi,gfke->gkie", incoming.astype(jnp.float32), gathered.astype(jnp.float32))
    weighted = 2.0 * jnp.sum(pair_grad * slopes, axis=1) * keep_mask
    row_grad = jnp.sum(separation * weighted[:, None, :, :], axis=3)
    column_grad = -jnp.sum(separation * weighted[:, None, :, :], axis=2)
    return summed.at[row_index].add(row_grad).at[column_index].add(column_grad)


def tile_window(local_list, extended_list, first_tile, stop_tile, round_index):
    position = first_tile + round_index * GROUP + jnp.arange(GROUP, dtype=jnp.int32)
    weight = (position < stop_tile).astype(jnp.float32)
    clipped = jnp.minimum(position, local_list.shape[0] - 1)
    return jnp.take(local_list, clipped), jnp.take(extended_list, clipped), weight


def sweep(update, initial, local_list, extended_list, first_tile, stop_tile, row_base, column_base):
    rounds = (stop_tile - first_tile + GROUP - 1) // GROUP

    def advance(round_index, carried):
        local_rows, extended_columns, weight = tile_window(local_list, extended_list, first_tile, stop_tile, round_index)
        same_block = (extended_columns == local_rows + CELLS).astype(jnp.float32)
        return update(carried, local_rows + row_base, extended_columns + column_base, local_rows, same_block, weight)

    return lax.fori_loop(0, rounds, advance, initial)


def project(feature_blocks, msg_weight):
    tables = jnp.einsum("kgf,nfa->ngka", msg_weight.astype(jnp.float32), feature_blocks, precision=lax.Precision.HIGHEST)
    return tables.astype(jnp.bfloat16)


def node_backward(message, own_features, occupied, update_weight, mix_weight, out_weight):
    scaled = (message * MESSAGE_SCALE).astype(jnp.bfloat16)
    first_pre = jnp.einsum("gf,cfa->cga", update_weight.astype(jnp.float32), scaled.astype(jnp.float32))
    first_gate = jax.nn.sigmoid(first_pre)
    updated = (own_features + first_pre * first_gate).astype(jnp.bfloat16)
    second_pre = jnp.einsum("gf,cfa->cga", mix_weight.astype(jnp.float32), updated.astype(jnp.float32))
    second_gate = jax.nn.sigmoid(second_pre)
    second_grad = (out_weight.astype(jnp.float32)[None, :, None] * second_gate * (1.0 + second_pre * (1.0 - second_gate)) * occupied[:, None, :]).astype(jnp.bfloat16)
    update_grad = jnp.einsum("gf,cga->cfa", mix_weight.astype(jnp.float32), second_grad.astype(jnp.float32))
    first_grad = (update_grad * first_gate * (1.0 + first_pre * (1.0 - first_gate))).astype(jnp.bfloat16)
    return (MESSAGE_SCALE * jnp.einsum("gf,cga->cfa", update_weight.astype(jnp.float32), first_grad.astype(jnp.float32))).astype(jnp.bfloat16)


def reference(positions, momenta, features, masses, radial_width, msg_weight, update_weight, mix_weight, out_weight, counts, pairs, npairs, leaving):
    slot_index = jnp.arange(BLK, dtype=jnp.int32)
    occupied = (slot_index[None, None, :] < counts.reshape(DOMAINS, CELLS, 1)).astype(jnp.float32)
    feature_blocks = jnp.transpose(features.reshape(F, DOMAINS, CELLS, BLK), (1, 2, 0, 3)) * occupied[:, :, None, :]
    tables = project(feature_blocks.reshape(DOMAINS * CELLS, F, BLK), msg_weight).reshape(DOMAINS, CELLS, F, RAD, BLK)
    table_ext = jnp.concatenate([jnp.roll(tables, 1, axis=0), tables, jnp.roll(tables, -1, axis=0)], axis=1)
    coords = jnp.transpose(positions.reshape(BEADS, 3, DOMAINS, CELLS, BLK), (0, 2, 3, 1, 4))
    vertical = jnp.array([0.0, 0.0, CELL_SIDE], dtype=jnp.float32)[:, None]
    coord_ext = jnp.concatenate([jnp.roll(coords, 1, axis=1) - vertical, coords, jnp.roll(coords, -1, axis=1) + vertical], axis=2)
    inverse_width = 1.0 / (radial_width * radial_width)
    local_lists = pairs[0].reshape(DOMAINS, PMAX)
    extended_lists = pairs[1].reshape(DOMAINS, PMAX)

    def one_domain(domain):
        local_list = local_lists[domain]
        extended_list = extended_lists[domain]
        tile_count = npairs[domain]
        table_here = table_ext[domain]
        own_features = feature_blocks[domain]
        own_occupied = occupied[domain]

        def one_bead(coord_here):
            message = sweep(partial(message_group, coord_here, table_here, inverse_width), jnp.zeros((CELLS, F, BLK), jnp.float32), local_list, extended_list, 0, tile_count, CELLS, 0)
            downstream = node_backward(message, own_features, own_occupied, update_weight, mix_weight, out_weight)
            return sweep(partial(force_group, coord_here, table_here, downstream, inverse_width), jnp.zeros((3 * CELLS, 3, BLK), jnp.float32), local_list, extended_list, 0, tile_count, CELLS, 0)

        return jax.vmap(one_bead)(coord_ext[:, domain])

    gradients = lax.map(one_domain, jnp.arange(DOMAINS, dtype=jnp.int32))
    own_grad = gradients[:, :, CELLS:2 * CELLS] + jnp.roll(gradients[:, :, 2 * CELLS:], 1, axis=0) + jnp.roll(gradients[:, :, :CELLS], -1, axis=0)
    physical = -jnp.transpose(own_grad, (1, 3, 0, 2, 4)).reshape(BEADS, 3, ATOMS)
    spring = -SPRING_RATE * masses[None, None, :] * (2.0 * positions - jnp.roll(positions, 1, axis=0) - jnp.roll(positions, -1, axis=0))
    forces = physical + spring
    momenta_new = momenta + forces
    positions_new = positions + momenta_new / masses[None, None, :]
    packet = jnp.concatenate([positions_new, momenta_new], axis=1).reshape(BEADS, 6, DOMAINS, ATOMS_DEV)
    movers = jnp.transpose(leaving.reshape(2, DOMAINS, MIG), (1, 0, 2)).reshape(DOMAINS, 2 * MIG)
    present = (movers >= 0).astype(jnp.float32)
    picked = jnp.take_along_axis(packet, jnp.broadcast_to(jnp.maximum(movers, 0)[None, None], (BEADS, 6, DOMAINS, 2 * MIG)), axis=3)
    face_shift = jnp.where(jnp.arange(2 * MIG) < MIG, CELL_SIDE, -CELL_SIDE)
    height_row = (jnp.arange(6) == 2).astype(jnp.float32)
    picked = (picked + height_row[None, :, None, None] * face_shift[None, None, None, :]) * present[None, None]
    arrivals = jnp.concatenate([jnp.roll(picked[:, :, :, MIG:], 1, axis=2), jnp.roll(picked[:, :, :, :MIG], -1, axis=2)], axis=3).reshape(BEADS, 6, DOMAINS * 2 * MIG)
    return forces, positions_new, momenta_new, arrivals
```

```python
from functools import partial

import jax
import jax.numpy as jnp
from jax import lax
from jax.experimental import pallas as pl
from jax.experimental.pallas import tpu as pltpu
from jax.sharding import PartitionSpec as P

F = 64
RAD = 4
BLK = 128
MIG = 64
CELLS = 8
ATOMS_DEV = CELLS * BLK
PACK = 72

CUTOFF_SQUARE = 36.0
CELL_SIDE = 10.0
MESSAGE_SCALE = 0.25
SPRING_RATE = 0.2
LOG2E = 1.4426950408889634
FAR = 1.0e9
CHUNK = 16

f32 = jnp.float32
bf16 = jnp.bfloat16
VMEM = pl.BlockSpec(memory_space=pltpu.VMEM)
SMEM = pl.BlockSpec(memory_space=pltpu.SMEM)
PARAMS = pltpu.CompilerParams(vmem_limit_bytes=48 * 1024 * 1024)


def dot(a, b, dims=((1,), (0,))):
    return lax.dot_general(a, b, (dims, ((), ())), preferred_element_type=f32)


def halves(x):
    high = x.astype(bf16)
    return high, (x - high.astype(f32)).astype(bf16)


def block_lanes(x, b):
    return x[:, b * BLK : (b + 1) * BLK]


def pack_kernel(features, positions, counts, packed):
    lane = lax.broadcasted_iota(jnp.int32, (1, BLK), 1)
    for b in range(CELLS):
        cols = slice(b * BLK, (b + 1) * BLK)
        keep = (lane < counts[b]).astype(f32)
        packed[0:F, cols] = features[:, cols] * keep
        packed[F : F + 3, cols] = positions[0, :, cols]
        packed[F + 3 : PACK, cols] = jnp.zeros((PACK - F - 3, BLK), f32)


def split_lists(pairs, npairs, own_list, ghost_list, tallies):
    def step(p, carry):
        own, ghost = carry
        i = pairs[0, p]
        j = pairs[1, p]
        mine = jnp.logical_and(j >= CELLS, j < 2 * CELLS)
        shifted = jnp.where(mine, j - CELLS, jnp.where(j >= 2 * CELLS, j - CELLS, j))
        code = i * 16 + shifted
        own_list[own] = code
        ghost_list[ghost] = code
        taken = mine.astype(jnp.int32)
        return own + taken, ghost + 1 - taken

    own, ghost = lax.fori_loop(0, npairs[0], step, (jnp.int32(0), jnp.int32(0)))
    for extra in range(4):
        own_list[own + extra] = CELLS * 16
        ghost_list[ghost + extra] = CELLS * 16
    tallies[0] = own
    tallies[1] = ghost


def fill_tables(packed, weight, tables, base):
    high, low = halves(packed[0:F, :])
    stacked = jnp.concatenate([high, low], axis=0)
    result = dot(weight, stacked)
    for b in range(CELLS):
        for k in range(RAD):
            tables[base + b, :, k * BLK : (k + 1) * BLK] = block_lanes(
                result[k * F : (k + 1) * F], b
            ).astype(bf16)


def fill_transposed(packed, turned, base):
    x = packed[0:F, :]
    high = x.astype(bf16).astype(f32)
    stacked = jnp.concatenate([high, x - high], axis=0)
    for b in range(CELLS):
        turned[base + b] = block_lanes(stacked, b).T.astype(bf16)


def fill_rows(packed, rows):
    for b in range(CELLS):
        rows[b, 0:3, :] = packed[F : F + 3, b * BLK : (b + 1) * BLK]
    rows[CELLS] = jnp.zeros((8, BLK), f32)


def fill_columns(sources, columns):
    pieces = []
    for packed, shift in sources:
        third = lax.broadcasted_iota(jnp.int32, (3, BLK), 0) == 2
        for b in range(CELLS):
            piece = packed[F : F + 3, b * BLK : (b + 1) * BLK]
            if shift:
                piece = piece + jnp.where(third, shift, 0.0)
            pieces.append(piece)
    used = 3 * len(pieces)
    pieces.append(jnp.zeros((BLK - used, BLK), f32))
    turned = jnp.concatenate(pieces, axis=0).T
    for n in range(used):
        columns[n // 3, n % 3] = jnp.broadcast_to(turned[:, n : n + 1], (BLK, BLK))


def fill_penalty(penalty):
    same = lax.broadcasted_iota(jnp.int32, (BLK, BLK), 0) == lax.broadcasted_iota(
        jnp.int32, (BLK, BLK), 1
    )
    penalty[0] = jnp.zeros((BLK, BLK), f32)
    penalty[1] = jnp.where(same, FAR, 0.0)


def inverse_widths(radial_width):
    return [1.0 / (radial_width[k] * radial_width[k]) for k in range(RAD)]


def decode(pair_list, p):
    code = pair_list[p]
    return lax.shift_right_logical(code, 4), lax.bitwise_and(code, 15)


def separation(rows, columns, penalty, i, j, place):
    parts = [rows[i, c : c + 1, :] - columns[j, c, place, :] for c in range(3)]
    squared = parts[0] * parts[0] + parts[1] * parts[1] + parts[2] * parts[2]
    if penalty is not None:
        squared = squared + penalty[(i == j).astype(jnp.int32), place, :]
    remain = jnp.maximum(1.0 - squared * (1.0 / CUTOFF_SQUARE), 0.0)
    return parts, squared, remain


def message_pass(pair_list, count, rows, columns, penalty, rates, tables, amps, message):
    def amplitudes(p, amp):
        i, j = decode(pair_list, p)
        for r in range(BLK // CHUNK):
            place = slice(r * CHUNK, (r + 1) * CHUNK)
            _, squared, remain = separation(rows, columns, penalty, i, j, place)
            cutoff = remain * remain
            for k in range(RAD):
                value = jnp.exp2(squared * rates[k]) * cutoff
                amp[k * BLK + r * CHUNK : k * BLK + (r + 1) * CHUNK, :] = value.astype(bf16)

    def multiply(p, amp):
        i, j = decode(pair_list, p)
        message[i] += dot(tables[j], amp[...])

    amp_a, amp_b = amps

    @pl.when(count > 0)
    def _():
        amplitudes(0, amp_a)

    def step(t, carry):
        multiply(2 * t, amp_a)
        amplitudes(2 * t + 1, amp_b)
        multiply(2 * t + 1, amp_b)
        amplitudes(2 * t + 2, amp_a)
        return carry

    lax.fori_loop(0, (count + 1) // 2, step, 0)


def force_pass(
    pair_list, count, rows, columns, penalty, rates, doubled, turned, down, grads, row_sum, column_sum
):
    lane = lax.broadcasted_iota(jnp.int32, (CHUNK, BLK), 1)

    def products(p, grad):
        i, j = decode(pair_list, p)
        right = down[i]
        grad[...] = dot(turned[j], jnp.concatenate([right, right], axis=0))

    def apply(p, grad):
        i, j = decode(pair_list, p)
        marks = [lane == 3 * j + c for c in range(3)]
        sums = [jnp.zeros((CHUNK, BLK), f32) for _ in range(3)]
        for r in range(BLK // CHUNK):
            place = slice(r * CHUNK, (r + 1) * CHUNK)
            parts, squared, remain = separation(rows, columns, penalty, i, j, place)
            plain = None
            scaled = None
            for k in range(RAD):
                term = jnp.exp2(squared * rates[k]) * grad[place, k * BLK : (k + 1) * BLK]
                plain = term if plain is None else plain + term
                term = term * doubled[k]
                scaled = term if scaled is None else scaled + term
            weighted = remain * (plain + remain * scaled)
            pulls = [weighted * part for part in parts]
            sums = [s + pull for s, pull in zip(sums, pulls)]
            totals = [jnp.sum(pull, axis=1, keepdims=True) for pull in pulls]
            placed = jnp.where(
                marks[0],
                totals[0],
                jnp.where(marks[1], totals[1], jnp.where(marks[2], totals[2], 0.0)),
            )
            column_sum[place, :] += placed
        for c in range(3):
            row_sum[i, c] += sums[c]

    grad_a, grad_b = grads

    @pl.when(count > 0)
    def _():
        products(0, grad_a)

    def step(t, carry):
        products(2 * t + 1, grad_b)
        apply(2 * t, grad_a)
        products(2 * t + 2, grad_a)
        apply(2 * t + 1, grad_b)
        return carry

    lax.fori_loop(0, (count + 1) // 2, step, 0)


def own_message_kernel(
    packed,
    pairs,
    npairs,
    radial_width,
    weight,
    message,
    own_list,
    ghost_list,
    tallies,
    tables,
    rows,
    columns,
    penalty,
    amp_a,
    amp_b,
):
    split_lists(pairs, npairs, own_list, ghost_list, tallies)
    fill_tables(packed, jnp.concatenate([weight[...], weight[...]], axis=1), tables, 0)
    fill_rows(packed, rows)
    fill_columns([(packed, 0.0)], columns)
    fill_penalty(penalty)
    message[...] = jnp.zeros(message.shape, f32)
    rates = [-LOG2E * inverse for inverse in inverse_widths(radial_width)]
    message_pass(
        own_list, tallies[0], rows, columns, penalty, rates, tables, (amp_a, amp_b), message
    )


def node_backward(
    message, packed, counts, weight, update_weight, mix_weight, out_weight, down
):
    whole = jnp.concatenate([message[b] for b in range(CELLS)], axis=1)
    scaled = (whole * MESSAGE_SCALE).astype(bf16)
    first_pre = dot(update_weight[...], scaled)
    first_gate = jax.nn.sigmoid(first_pre)
    updated = (packed[0:F, :] + first_pre * first_gate).astype(bf16)
    second_pre = dot(mix_weight[...], updated)
    second_gate = jax.nn.sigmoid(second_pre)
    lane = lax.broadcasted_iota(jnp.int32, (1, BLK), 1)
    occupied = jnp.concatenate([(lane < counts[b]).astype(f32) for b in range(CELLS)], axis=1)
    second_grad = (
        out_weight[...].astype(f32)
        * second_gate
        * (1.0 + second_pre * (1.0 - second_gate))
        * occupied
    ).astype(bf16)
    update_grad = dot(mix_weight[...], second_grad, ((0,), (0,)))
    first_grad = (update_grad * first_gate * (1.0 + first_pre * (1.0 - first_gate))).astype(bf16)
    downstream = (MESSAGE_SCALE * dot(update_weight[...], first_grad, ((0,), (0,)))).astype(bf16)
    for k in range(RAD):
        mixed = dot(weight[k * F : (k + 1) * F, :], downstream, ((0,), (0,)))
        mixed = (mixed * (4.0 / CUTOFF_SQUARE)).astype(bf16)
        for b in range(CELLS):
            down[b, :, k * BLK : (k + 1) * BLK] = block_lanes(mixed, b)
    down[CELLS] = jnp.zeros((F, RAD * BLK), bf16)


def doubled_rates(inverse):
    return [value * (0.5 * CUTOFF_SQUARE) for value in inverse]


def collect_rows(row_sum, out, start=None):
    for b in range(CELLS):
        for c in range(3):
            total = jnp.sum(row_sum[b, c], axis=0, keepdims=True)
            n = 3 * b + c
            out[n : n + 1, :] = total if start is None else total + start[n : n + 1, :]


def ghost_kernel(
    packed,
    below,
    above,
    own_message,
    ghost_list,
    tallies,
    counts,
    radial_width,
    weight,
    update_weight,
    mix_weight,
    out_weight,
    row_force,
    ghost_below,
    ghost_above,
    down,
    message,
    tables,
    turned,
    rows,
    columns,
    amp_a,
    amp_b,
    grad_a,
    grad_b,
    row_sum,
    column_sum,
):
    doubled_weight = jnp.concatenate([weight[...], weight[...]], axis=1)
    fill_tables(below, doubled_weight, tables, 0)
    fill_tables(above, doubled_weight, tables, CELLS)
    fill_rows(packed, rows)
    fill_columns([(below, -CELL_SIDE), (above, CELL_SIDE)], columns)
    message[...] = own_message[...]
    inverse = inverse_widths(radial_width)
    rates = [-LOG2E * value for value in inverse]
    count = tallies[1]
    message_pass(
        ghost_list, count, rows, columns, None, rates, tables, (amp_a, amp_b), message
    )
    fill_transposed(below, turned, 0)
    fill_transposed(above, turned, CELLS)
    node_backward(message, packed, counts, weight, update_weight, mix_weight, out_weight, down)
    row_sum[...] = jnp.zeros(row_sum.shape, f32)
    column_sum[...] = jnp.zeros(column_sum.shape, f32)
    force_pass(
        ghost_list,
        count,
        rows,
        columns,
        None,
        rates,
        doubled_rates(inverse),
        turned,
        down,
        (grad_a, grad_b),
        row_sum,
        column_sum,
    )
    collect_rows(row_sum, row_force)
    flat = column_sum[...].T
    ghost_below[...] = flat[0:24]
    ghost_above[...] = flat[24:48]


def own_force_kernel(
    packed,
    row_force,
    down,
    own_list,
    tallies,
    radial_width,
    force,
    turned,
    rows,
    columns,
    penalty,
    grad_a,
    grad_b,
    row_sum,
    column_sum,
):
    fill_rows(packed, rows)
    fill_columns([(packed, 0.0)], columns)
    fill_penalty(penalty)
    fill_transposed(packed, turned, 0)
    row_sum[...] = jnp.zeros(row_sum.shape, f32)
    column_sum[...] = jnp.zeros(column_sum.shape, f32)
    inverse = inverse_widths(radial_width)
    rates = [-LOG2E * value for value in inverse]
    force_pass(
        own_list,
        tallies[0],
        rows,
        columns,
        penalty,
        rates,
        doubled_rates(inverse),
        turned,
        down,
        (grad_a, grad_b),
        row_sum,
        column_sum,
    )
    collect_rows(row_sum, force, row_force[...] - column_sum[...].T[0:24])


def finish_kernel(
    force,
    from_above,
    from_below,
    positions,
    momenta,
    before,
    after,
    masses,
    leaving,
    forces,
    positions_new,
    momenta_new,
    upward,
    downward,
):
    pair_force = force[...] - from_above[...] - from_below[...]
    physical = jnp.concatenate([pair_force[3 * b : 3 * b + 3, :] for b in range(CELLS)], axis=1)
    mass = masses[...]
    current = positions[0]
    spring = -SPRING_RATE * mass * (2.0 * current - before[0] - after[0])
    total = physical + spring
    moved = momenta[0] + total
    placed = current + moved / mass
    forces[0] = total
    momenta_new[0] = moved
    positions_new[0] = placed
    movers = jnp.concatenate([leaving[1:2, :], leaving[0:1, :]], axis=1)
    slot = lax.broadcasted_iota(jnp.int32, (ATOMS_DEV, 2 * MIG), 0)
    chosen = (slot == movers).astype(f32).astype(bf16)
    packet = jnp.concatenate([placed, moved, jnp.zeros((2, ATOMS_DEV), f32)], axis=0)
    high = packet.astype(bf16)
    middle, third = halves(packet - high.astype(f32))
    picked = dot(high, chosen) + (dot(middle, chosen) + dot(third, chosen))
    lane = lax.broadcasted_iota(jnp.int32, (8, 2 * MIG), 1)
    row = lax.broadcasted_iota(jnp.int32, (8, 2 * MIG), 0)
    shift = jnp.where(lane < MIG, -CELL_SIDE, CELL_SIDE)
    present = movers >= 0
    shifted = jnp.where(present, picked + jnp.where(row == 2, shift, 0.0), 0.0)
    upward[0] = jnp.where(lane < MIG, shifted, 0.0)[0:6]
    downward[0] = jnp.where(lane < MIG, 0.0, shifted)[0:6]


def shape(dims, kind=f32):
    return jax.ShapeDtypeStruct(dims, kind)


def body(
    positions,
    momenta,
    features,
    masses,
    radial_width,
    msg_weight,
    update_weight,
    mix_weight,
    out_weight,
    counts,
    pairs,
    npairs,
    leaving,
):
    def ring(axis, step):
        count = lax.axis_size(axis)
        return [(i, (i + step) % count) for i in range(count)]

    weight = msg_weight.reshape(RAD * F, F)
    packed = pl.pallas_call(
        pack_kernel,
        out_shape=shape((PACK, ATOMS_DEV)),
        in_specs=[VMEM, VMEM, SMEM],
        out_specs=VMEM,
        compiler_params=PARAMS,
    )(features, positions, counts)
    below = lax.ppermute(packed, "dom", ring("dom", 1))
    above = lax.ppermute(packed, "dom", ring("dom", -1))
    before = lax.ppermute(positions, "bead", ring("bead", 1))
    after = lax.ppermute(positions, "bead", ring("bead", -1))

    amp = pltpu.VMEM((RAD * BLK, BLK), bf16)
    grad = pltpu.VMEM((BLK, RAD * BLK), f32)
    rows = pltpu.VMEM((CELLS + 1, 8, BLK), f32)
    row_sum = pltpu.VMEM((CELLS + 1, 3, CHUNK, BLK), f32)
    column_sum = pltpu.VMEM((BLK, BLK), f32)
    penalty = pltpu.VMEM((2, BLK, BLK), f32)
    listed = shape((pairs.shape[1] + 8,), jnp.int32)

    def columns(blocks):
        return pltpu.VMEM((blocks, 3, BLK, BLK), f32)

    def tables(blocks):
        return pltpu.VMEM((blocks, F, RAD * BLK), bf16)

    def turned(blocks):
        return pltpu.VMEM((blocks, BLK, BLK), bf16)

    own_message, own_list, ghost_list, tallies = pl.pallas_call(
        own_message_kernel,
        out_shape=(shape((CELLS + 1, F, BLK)), listed, listed, shape((2,), jnp.int32)),
        in_specs=[VMEM, SMEM, SMEM, SMEM, VMEM],
        out_specs=(VMEM, SMEM, SMEM, SMEM),
        scratch_shapes=[tables(CELLS), rows, columns(CELLS), penalty, amp, amp],
        compiler_params=PARAMS,
    )(packed, pairs, npairs, radial_width, weight)
    row_force, ghost_below, ghost_above, down = pl.pallas_call(
        ghost_kernel,
        out_shape=(
            shape((24, BLK)),
            shape((24, BLK)),
            shape((24, BLK)),
            shape((CELLS + 1, F, RAD * BLK), bf16),
        ),
        in_specs=[VMEM] * 4 + [SMEM] * 4 + [VMEM] * 4,
        out_specs=(VMEM,) * 4,
        scratch_shapes=[
            pltpu.VMEM((CELLS + 1, F, BLK), f32),
            tables(2 * CELLS),
            turned(2 * CELLS),
            rows,
            columns(2 * CELLS),
            amp,
            amp,
            grad,
            grad,
            row_sum,
            column_sum,
        ],
        compiler_params=PARAMS,
    )(
        packed,
        below,
        above,
        own_message,
        ghost_list,
        tallies,
        counts,
        radial_width,
        weight,
        update_weight,
        mix_weight,
        out_weight.reshape(F, 1),
    )
    from_above = lax.ppermute(ghost_below, "dom", ring("dom", -1))
    from_below = lax.ppermute(ghost_above, "dom", ring("dom", 1))
    force = pl.pallas_call(
        own_force_kernel,
        out_shape=shape((24, BLK)),
        in_specs=[VMEM] * 3 + [SMEM] * 3,
        out_specs=VMEM,
        scratch_shapes=[
            turned(CELLS),
            rows,
            columns(CELLS),
            penalty,
            grad,
            grad,
            row_sum,
            column_sum,
        ],
        compiler_params=PARAMS,
    )(packed, row_force, down, own_list, tallies, radial_width)
    whole = shape((1, 3, ATOMS_DEV))
    packet = shape((1, 6, 2 * MIG))
    forces, positions_new, momenta_new, upward, downward = pl.pallas_call(
        finish_kernel,
        out_shape=(whole, whole, whole, packet, packet),
        in_specs=[VMEM] * 9,
        out_specs=(VMEM,) * 5,
        compiler_params=PARAMS,
    )(
        force,
        from_above,
        from_below,
        positions,
        momenta,
        before,
        after,
        masses.reshape(1, ATOMS_DEV),
        leaving,
    )
    arrivals = lax.ppermute(upward, "dom", ring("dom", 1)) + lax.ppermute(
        downward, "dom", ring("dom", -1)
    )
    return forces, positions_new, momenta_new, arrivals


def solution(mesh):
    split = P("bead", None, "dom")
    in_specs = (
        split,
        split,
        P(None, "dom"),
        P("dom"),
        P(),
        P(),
        P(),
        P(),
        P(),
        P("dom"),
        P(None, "dom"),
        P("dom"),
        P(None, "dom"),
    )
    out_specs = (split, split, split, split)
    return jax.shard_map(body, mesh=mesh, in_specs=in_specs, out_specs=out_specs, check_vma=False)
```

```python
from functools import partial

import jax
import jax.numpy as jnp
from jax import lax
from jax.experimental import pallas as pl
from jax.experimental.pallas import tpu as pltpu
from jax.sharding import PartitionSpec as P

F = 64
RAD = 4
BLK = 128
MIG = 64
CELLS = 8
ATOMS_DEV = CELLS * BLK
PACK = 72

CUTOFF_SQUARE = 36.0
CELL_SIDE = 10.0
MESSAGE_SCALE = 0.25
SPRING_RATE = 0.2
LOG2E = 1.4426950408889634
FAR = 1.0e9
CHUNK = 16
GROUP = 4

f32 = jnp.float32
bf16 = jnp.bfloat16
VMEM = pl.BlockSpec(memory_space=pltpu.VMEM)
SMEM = pl.BlockSpec(memory_space=pltpu.SMEM)
PARAMS = pltpu.CompilerParams(vmem_limit_bytes=48 * 1024 * 1024)


def dot(a, b, dims=((1,), (0,))):
    return lax.dot_general(a, b, (dims, ((), ())), preferred_element_type=f32)


def halves(x):
    high = x.astype(bf16)
    return high, (x - high.astype(f32)).astype(bf16)


def block_lanes(x, b):
    return x[:, b * BLK : (b + 1) * BLK]


def pack_kernel(features, positions, counts, packed):
    lane = lax.broadcasted_iota(jnp.int32, (1, BLK), 1)
    for b in range(CELLS):
        keep = (lane < counts[b]).astype(f32)
        packed[b, 0:F, :] = features[:, b * BLK : (b + 1) * BLK] * keep
        place = [positions[c * CELLS + b : c * CELLS + b + 1, :] for c in range(3)]
        packed[b, F:PACK, :] = jnp.concatenate(place + [jnp.zeros((5, BLK), f32)], axis=0)


def split_lists(pairs, npairs, own_list, ghost_list, tallies):
    def step(p, carry):
        own, ghost = carry
        i = pairs[0, p]
        j = pairs[1, p]
        mine = jnp.logical_and(j >= CELLS, j < 2 * CELLS)
        shifted = jnp.where(mine, j - CELLS, jnp.where(j >= 2 * CELLS, j - CELLS, j))
        code = i * 16 + shifted
        own_list[own] = code
        ghost_list[ghost] = code
        taken = mine.astype(jnp.int32)
        return own + taken, ghost + 1 - taken

    own, ghost = lax.fori_loop(0, npairs[0], step, (jnp.int32(0), jnp.int32(0)))
    for extra in range(2 * GROUP):
        own_list[own + extra] = CELLS * 16
        ghost_list[ghost + extra] = CELLS * 16
    tallies[0] = own
    tallies[1] = ghost


def feature_rows(packed):
    return jnp.concatenate([packed[b, 0:F, :] for b in range(CELLS)], axis=1)


def fill_tables(packed, weight, tables, base):
    high, low = halves(feature_rows(packed))
    stacked = jnp.concatenate([high, low], axis=0)
    result = dot(weight, stacked)
    for b in range(CELLS):
        for k in range(RAD):
            tables[base + b, :, k * BLK : (k + 1) * BLK] = block_lanes(
                result[k * F : (k + 1) * F], b
            ).astype(bf16)


def fill_transposed(packed, turned, base):
    for b in range(CELLS):
        x = packed[b, 0:F, :]
        high = x.astype(bf16).astype(f32)
        stacked = jnp.concatenate([high, x - high], axis=0)
        turned[base + b] = stacked.T.astype(bf16)


def fill_columns(sources, columns):
    pieces = []
    for packed, shift in sources:
        for b in range(CELLS):
            piece = packed[b, F:PACK, :]
            if shift:
                third = lax.broadcasted_iota(jnp.int32, (PACK - F, BLK), 0) == 2
                piece = piece + jnp.where(third, shift, 0.0)
            pieces.append(piece)
    blocks = len(pieces)
    width = PACK - F
    if width * blocks < BLK:
        pieces.append(jnp.zeros((BLK - width * blocks, BLK), f32))
    turned = jnp.concatenate(pieces, axis=0).T
    for b in range(blocks):
        for c in range(3):
            n = width * b + c
            columns[b, c] = jnp.broadcast_to(turned[:, n : n + 1], (BLK, BLK))


def fill_penalty(penalty):
    same = lax.broadcasted_iota(jnp.int32, (BLK, BLK), 0) == lax.broadcasted_iota(
        jnp.int32, (BLK, BLK), 1
    )
    penalty[0] = jnp.zeros((BLK, BLK), f32)
    penalty[1] = jnp.where(same, FAR, 0.0)


def inverse_widths(radial_width):
    return [1.0 / (radial_width[k] * radial_width[k]) for k in range(RAD)]


def decode(pair_list, p):
    code = pair_list[p]
    return lax.shift_right_logical(code, 4), lax.bitwise_and(code, 15)


def separation(packed, columns, penalty, i, j, place):
    parts = [packed[i & 7, F + c : F + c + 1, :] - columns[j, c, place, :] for c in range(3)]
    squared = parts[0] * parts[0] + parts[1] * parts[1] + parts[2] * parts[2]
    if penalty is not None:
        squared = squared + penalty[(i == j).astype(jnp.int32), place, :]
    remain = jnp.maximum(1.0 - squared * (1.0 / CUTOFF_SQUARE), 0.0)
    return parts, squared, remain


def message_pass(pair_list, count, packed, columns, penalty, rates, tables, amps, message):
    def amplitudes(p, amp):
        i, j = decode(pair_list, p)
        for r in range(BLK // CHUNK):
            place = slice(r * CHUNK, (r + 1) * CHUNK)
            _, squared, remain = separation(packed, columns, penalty, i, j, place)
            cutoff = remain * remain
            for k in range(RAD):
                value = jnp.exp2(squared * rates[k]) * cutoff
                amp[k * BLK + r * CHUNK : k * BLK + (r + 1) * CHUNK, :] = value.astype(bf16)

    def multiply(p, amp):
        i, j = decode(pair_list, p)
        message[i] += dot(tables[j], amp[...])

    @pl.when(count > 0)
    def _():
        for u, amp in enumerate(amps):
            amplitudes(u, amp)

    def step(t, carry):
        for u, amp in enumerate(amps):
            multiply(GROUP * t + u, amp)
        for u, amp in enumerate(amps):
            amplitudes(GROUP * t + GROUP + u, amp)
        return carry

    lax.fori_loop(0, (count + GROUP - 1) // GROUP, step, 0)


def force_pass(
    pair_list, count, packed, columns, penalty, rates, doubled, turned, down, grads, row_sum, column_sum
):
    lane = lax.broadcasted_iota(jnp.int32, (CHUNK, BLK), 1)

    def products(p, grad):
        i, j = decode(pair_list, p)
        right = down[i]
        grad[...] = dot(turned[j], jnp.concatenate([right, right], axis=0))

    def apply(p, grad):
        i, j = decode(pair_list, p)
        marks = [lane == 3 * j + c for c in range(3)]
        sums = [jnp.zeros((CHUNK, BLK), f32) for _ in range(3)]
        for r in range(BLK // CHUNK):
            place = slice(r * CHUNK, (r + 1) * CHUNK)
            parts, squared, remain = separation(packed, columns, penalty, i, j, place)
            plain = None
            scaled = None
            for k in range(RAD):
                term = jnp.exp2(squared * rates[k]) * grad[place, k * BLK : (k + 1) * BLK]
                plain = term if plain is None else plain + term
                term = term * doubled[k]
                scaled = term if scaled is None else scaled + term
            weighted = remain * (plain + remain * scaled)
            pulls = [weighted * part for part in parts]
            sums = [s + pull for s, pull in zip(sums, pulls)]
            totals = [jnp.sum(pull, axis=1, keepdims=True) for pull in pulls]
            placed = jnp.where(
                marks[0],
                totals[0],
                jnp.where(marks[1], totals[1], jnp.where(marks[2], totals[2], 0.0)),
            )
            column_sum[place, :] += placed
        for c in range(3):
            row_sum[i, c] += sums[c]

    pairs_each = GROUP // 2
    first, second = grads[:pairs_each], grads[pairs_each:]

    @pl.when(count > 0)
    def _():
        for u, grad in enumerate(first):
            products(u, grad)

    def step(t, carry):
        base = GROUP * t
        for u, grad in enumerate(second):
            products(base + pairs_each + u, grad)
        for u, grad in enumerate(first):
            apply(base + u, grad)
        for u, grad in enumerate(first):
            products(base + GROUP + u, grad)
        for u, grad in enumerate(second):
            apply(base + pairs_each + u, grad)
        return carry

    lax.fori_loop(0, (count + GROUP - 1) // GROUP, step, 0)


def own_message_kernel(
    packed,
    pairs,
    npairs,
    radial_width,
    weight,
    message,
    own_list,
    ghost_list,
    tallies,
    tables,
    columns,
    penalty,
    *amps,
):
    split_lists(pairs, npairs, own_list, ghost_list, tallies)
    fill_tables(packed, jnp.concatenate([weight[...], weight[...]], axis=1), tables, 0)
    fill_columns([(packed, 0.0)], columns)
    fill_penalty(penalty)
    message[...] = jnp.zeros(message.shape, f32)
    rates = [-LOG2E * inverse for inverse in inverse_widths(radial_width)]
    message_pass(own_list, tallies[0], packed, columns, penalty, rates, tables, amps, message)


def as_column(row):
    size = (row.shape[1], row.shape[1])
    diagonal = lax.broadcasted_iota(jnp.int32, size, 0) == lax.broadcasted_iota(jnp.int32, size, 1)
    return jnp.sum(jnp.where(diagonal, row, 0.0), axis=1, keepdims=True)


def node_backward(
    message, packed, counts, weight, update_weight, mix_weight, out_weight, down
):
    whole = jnp.concatenate([message[b] for b in range(CELLS)], axis=1)
    scaled = (whole * MESSAGE_SCALE).astype(bf16)
    first_pre = dot(update_weight[...], scaled)
    first_gate = jax.nn.sigmoid(first_pre)
    updated = (feature_rows(packed) + first_pre * first_gate).astype(bf16)
    second_pre = dot(mix_weight[...], updated)
    second_gate = jax.nn.sigmoid(second_pre)
    lane = lax.broadcasted_iota(jnp.int32, (1, BLK), 1)
    occupied = jnp.concatenate([(lane < counts[b]).astype(f32) for b in range(CELLS)], axis=1)
    second_grad = (
        as_column(out_weight[...].astype(f32))
        * second_gate
        * (1.0 + second_pre * (1.0 - second_gate))
        * occupied
    ).astype(bf16)
    update_grad = dot(mix_weight[...], second_grad, ((0,), (0,)))
    first_grad = (update_grad * first_gate * (1.0 + first_pre * (1.0 - first_gate))).astype(bf16)
    downstream = (MESSAGE_SCALE * dot(update_weight[...], first_grad, ((0,), (0,)))).astype(bf16)
    for k in range(RAD):
        mixed = dot(weight[k * F : (k + 1) * F, :], downstream, ((0,), (0,)))
        mixed = (mixed * (4.0 / CUTOFF_SQUARE)).astype(bf16)
        for b in range(CELLS):
            down[b, :, k * BLK : (k + 1) * BLK] = block_lanes(mixed, b)
    down[CELLS] = jnp.zeros((F, RAD * BLK), bf16)


def doubled_rates(inverse):
    return [value * (0.5 * CUTOFF_SQUARE) for value in inverse]


def collect_rows(row_sum, out, start=None):
    for b in range(CELLS):
        for c in range(3):
            total = jnp.sum(row_sum[b, c], axis=0, keepdims=True)
            n = CELLS * c + b
            m = 3 * b + c
            out[n : n + 1, :] = total if start is None else total - start[m : m + 1, :]


def ghost_kernel(
    packed,
    below,
    above,
    own_message,
    ghost_list,
    tallies,
    counts,
    radial_width,
    weight,
    update_weight,
    mix_weight,
    out_weight,
    row_force,
    ghost_below,
    ghost_above,
    down,
    message,
    tables,
    turned,
    columns,
    row_sum,
    column_sum,
    *buffers,
):
    amps, grads = buffers[:GROUP], buffers[GROUP:]
    doubled_weight = jnp.concatenate([weight[...], weight[...]], axis=1)
    fill_tables(below, doubled_weight, tables, 0)
    fill_tables(above, doubled_weight, tables, CELLS)
    fill_columns([(below, -CELL_SIDE), (above, CELL_SIDE)], columns)
    message[...] = own_message[...]
    inverse = inverse_widths(radial_width)
    rates = [-LOG2E * value for value in inverse]
    count = tallies[1]
    message_pass(ghost_list, count, packed, columns, None, rates, tables, amps, message)
    fill_transposed(below, turned, 0)
    fill_transposed(above, turned, CELLS)
    node_backward(message, packed, counts, weight, update_weight, mix_weight, out_weight, down)
    row_sum[...] = jnp.zeros(row_sum.shape, f32)
    column_sum[...] = jnp.zeros(column_sum.shape, f32)
    force_pass(
        ghost_list,
        count,
        packed,
        columns,
        None,
        rates,
        doubled_rates(inverse),
        turned,
        down,
        grads,
        row_sum,
        column_sum,
    )
    collect_rows(row_sum, row_force)
    flat = column_sum[...].T
    ghost_below[...] = flat[0:24]
    ghost_above[...] = flat[24:48]


def own_force_kernel(
    packed,
    row_force,
    down,
    own_list,
    tallies,
    radial_width,
    force,
    turned,
    columns,
    penalty,
    row_sum,
    column_sum,
    *grads,
):
    fill_columns([(packed, 0.0)], columns)
    fill_penalty(penalty)
    fill_transposed(packed, turned, 0)
    row_sum[...] = jnp.zeros(row_sum.shape, f32)
    column_sum[...] = jnp.zeros(column_sum.shape, f32)
    inverse = inverse_widths(radial_width)
    rates = [-LOG2E * value for value in inverse]
    force_pass(
        own_list,
        tallies[0],
        packed,
        columns,
        penalty,
        rates,
        doubled_rates(inverse),
        turned,
        down,
        grads,
        row_sum,
        column_sum,
    )
    collect_rows(row_sum, force, column_sum[...].T)
    force[...] += row_force[...]


def by_component(flat):
    return jnp.concatenate(
        [flat[3 * b + c : 3 * b + c + 1, :] for c in range(3) for b in range(CELLS)], axis=0
    )


def finish_kernel(
    force,
    from_above,
    from_below,
    positions,
    momenta,
    before,
    after,
    masses,
    leaving,
    forces,
    positions_new,
    momenta_new,
    upward,
    downward,
    packet,
):
    physical = force[...] - by_component(from_above[...] + from_below[...])
    mass = jnp.concatenate([masses[...]] * 3, axis=0)
    current = positions[...]
    spring = -SPRING_RATE * mass * (2.0 * current - before[...] - after[...])
    total = physical + spring
    moved = momenta[...] + total
    placed = current + moved / mass
    forces[...] = total
    momenta_new[...] = moved
    positions_new[...] = placed
    packet[0:24, :] = placed
    packet[24:48, :] = moved
    packet[48:64, :] = jnp.zeros((16, BLK), f32)
    movers = jnp.concatenate([leaving[1:2, :], leaving[0:1, :]], axis=1)
    slot = lax.broadcasted_iota(jnp.int32, (ATOMS_DEV, 2 * MIG), 0)
    chosen = (slot == movers).astype(f32).astype(bf16)
    values = jnp.concatenate([packet[pl.ds(b, 8, stride=CELLS), :] for b in range(CELLS)], axis=1)
    high = values.astype(bf16)
    middle, low = halves(values - high.astype(f32))
    picked = dot(high, chosen) + (dot(middle, chosen) + dot(low, chosen))
    lane = lax.broadcasted_iota(jnp.int32, (8, 2 * MIG), 1)
    row = lax.broadcasted_iota(jnp.int32, (8, 2 * MIG), 0)
    shift = jnp.where(lane < MIG, -CELL_SIDE, CELL_SIDE)
    shifted = jnp.where(movers >= 0, picked + jnp.where(row == 2, shift, 0.0), 0.0)
    up = jnp.where(lane < MIG, shifted, 0.0)
    down = jnp.where(lane < MIG, 0.0, shifted)
    for q in range(6):
        upward[q] = up[q : q + 1, :]
        downward[q] = down[q : q + 1, :]


def shape(dims, kind=f32):
    return jax.ShapeDtypeStruct(dims, kind)


def body(
    positions,
    momenta,
    features,
    masses,
    radial_width,
    msg_weight,
    update_weight,
    mix_weight,
    out_weight,
    counts,
    pairs,
    npairs,
    leaving,
):
    def ring(axis, step):
        count = lax.axis_size(axis)
        return [(i, (i + step) % count) for i in range(count)]

    weight = msg_weight.reshape(RAD * F, F)
    current = positions.reshape(3 * CELLS, BLK)
    packed = pl.pallas_call(
        pack_kernel,
        out_shape=shape((CELLS, PACK, BLK)),
        in_specs=[VMEM, VMEM, SMEM],
        out_specs=VMEM,
        compiler_params=PARAMS,
    )(features, current, counts)
    below = lax.ppermute(packed, "dom", ring("dom", 1))
    above = lax.ppermute(packed, "dom", ring("dom", -1))
    before = lax.ppermute(current, "bead", ring("bead", 1))
    after = lax.ppermute(current, "bead", ring("bead", -1))

    amp = pltpu.VMEM((RAD * BLK, BLK), bf16)
    grad = pltpu.VMEM((BLK, RAD * BLK), f32)
    row_sum = pltpu.VMEM((CELLS + 1, 3, CHUNK, BLK), f32)
    column_sum = pltpu.VMEM((BLK, BLK), f32)
    penalty = pltpu.VMEM((2, BLK, BLK), f32)
    listed = shape((pairs.shape[1] + 8,), jnp.int32)

    def columns(blocks):
        return pltpu.VMEM((blocks, 3, BLK, BLK), f32)

    def tables(blocks):
        return pltpu.VMEM((blocks, F, RAD * BLK), bf16)

    def turned(blocks):
        return pltpu.VMEM((blocks, BLK, BLK), bf16)

    own_message, own_list, ghost_list, tallies = pl.pallas_call(
        own_message_kernel,
        out_shape=(shape((CELLS + 1, F, BLK)), listed, listed, shape((2,), jnp.int32)),
        in_specs=[VMEM, SMEM, SMEM, SMEM, VMEM],
        out_specs=(VMEM, SMEM, SMEM, SMEM),
        scratch_shapes=[tables(CELLS), columns(CELLS), penalty] + [amp] * GROUP,
        compiler_params=PARAMS,
    )(packed, pairs, npairs, radial_width, weight)
    row_force, ghost_below, ghost_above, down = pl.pallas_call(
        ghost_kernel,
        out_shape=(
            shape((24, BLK)),
            shape((24, BLK)),
            shape((24, BLK)),
            shape((CELLS + 1, F, RAD * BLK), bf16),
        ),
        in_specs=[VMEM] * 4 + [SMEM] * 4 + [VMEM] * 4,
        out_specs=(VMEM,) * 4,
        scratch_shapes=[
            pltpu.VMEM((CELLS + 1, F, BLK), f32),
            tables(2 * CELLS),
            turned(2 * CELLS),
            columns(2 * CELLS),
            row_sum,
            column_sum,
        ]
        + [amp] * GROUP
        + [grad] * GROUP,
        compiler_params=PARAMS,
    )(
        packed,
        below,
        above,
        own_message,
        ghost_list,
        tallies,
        counts,
        radial_width,
        weight,
        update_weight,
        mix_weight,
        out_weight.reshape(1, F),
    )
    from_above = lax.ppermute(ghost_below, "dom", ring("dom", -1))
    from_below = lax.ppermute(ghost_above, "dom", ring("dom", 1))
    force = pl.pallas_call(
        own_force_kernel,
        out_shape=shape((24, BLK)),
        in_specs=[VMEM] * 3 + [SMEM] * 3,
        out_specs=VMEM,
        scratch_shapes=[
            turned(CELLS),
            columns(CELLS),
            penalty,
            row_sum,
            column_sum,
        ]
        + [grad] * GROUP,
        compiler_params=PARAMS,
    )(packed, row_force, down, own_list, tallies, radial_width)
    whole = shape((3 * CELLS, BLK))
    packet = shape((6, 1, 2 * MIG))
    forces, positions_new, momenta_new, upward, downward = pl.pallas_call(
        finish_kernel,
        out_shape=(whole, whole, whole, packet, packet),
        in_specs=[VMEM] * 9,
        out_specs=(VMEM,) * 5,
        scratch_shapes=[pltpu.VMEM((64, BLK), f32)],
        compiler_params=PARAMS,
    )(
        force,
        from_above,
        from_below,
        current,
        momenta.reshape(3 * CELLS, BLK),
        before,
        after,
        masses.reshape(CELLS, BLK),
        leaving,
    )
    arrivals = lax.ppermute(upward, "dom", ring("dom", 1)) + lax.ppermute(
        downward, "dom", ring("dom", -1)
    )
    result = tuple(x.reshape(1, 3, ATOMS_DEV) for x in (forces, positions_new, momenta_new))
    return result + (arrivals.reshape(1, 6, 2 * MIG),)


def solution(mesh):
    split = P("bead", None, "dom")
    in_specs = (
        split,
        split,
        P(None, "dom"),
        P("dom"),
        P(),
        P(),
        P(),
        P(),
        P(),
        P("dom"),
        P(None, "dom"),
        P("dom"),
        P(None, "dom"),
    )
    out_specs = (split, split, split, split)
    return jax.shard_map(body, mesh=mesh, in_specs=in_specs, out_specs=out_specs, check_vma=False)
```

```python
from functools import partial

import jax
import jax.numpy as jnp
from jax import lax
from jax.experimental import pallas as pl
from jax.experimental.pallas import tpu as pltpu
from jax.sharding import PartitionSpec as P

F = 64
RAD = 4
BLK = 128
MIG = 64
CELLS = 8
ATOMS_DEV = CELLS * BLK
PLACES = 3 * CELLS
SMALL = PLACES + CELLS

CUTOFF_SQUARE = 36.0
CELL_SIDE = 10.0
MESSAGE_SCALE = 0.25
SPRING_RATE = 0.2
LOG2E = 1.4426950408889634
FAR = 1.0e9
CHUNK = 16
GROUP = 4

f32 = jnp.float32
bf16 = jnp.bfloat16
VMEM = pl.BlockSpec(memory_space=pltpu.VMEM)
SMEM = pl.BlockSpec(memory_space=pltpu.SMEM)
PARAMS = pltpu.CompilerParams(vmem_limit_bytes=48 * 1024 * 1024)


def dot(a, b, dims=((1,), (0,))):
    return lax.dot_general(a, b, (dims, ((), ())), preferred_element_type=f32)


def halves(x):
    high = x.astype(bf16)
    return high, (x - high.astype(f32)).astype(bf16)


def block_lanes(x, b):
    return x[:, b * BLK : (b + 1) * BLK]


def pack_kernel(positions, counts, small):
    lane = lax.broadcasted_iota(jnp.int32, (1, BLK), 1)
    small[0:PLACES, :] = positions[...]
    for b in range(CELLS):
        small[PLACES + b : PLACES + b + 1, :] = (lane < counts[b]).astype(f32)


def occupancy(small):
    return jnp.concatenate([small[PLACES + b : PLACES + b + 1, :] for b in range(CELLS)], axis=1)


def split_lists(pairs, npairs, own_list, ghost_list, tallies):
    def step(p, carry):
        own, ghost = carry
        i = pairs[0, p]
        j = pairs[1, p]
        mine = jnp.logical_and(j >= CELLS, j < 2 * CELLS)
        shifted = jnp.where(mine, j - CELLS, jnp.where(j >= 2 * CELLS, j - CELLS, j))
        code = i * 16 + shifted
        own_list[own] = code
        ghost_list[ghost] = code
        taken = mine.astype(jnp.int32)
        return own + taken, ghost + 1 - taken

    own, ghost = lax.fori_loop(0, npairs[0], step, (jnp.int32(0), jnp.int32(0)))
    for extra in range(2 * GROUP):
        own_list[own + extra] = CELLS * 16
        ghost_list[ghost + extra] = CELLS * 16
    tallies[0] = own
    tallies[1] = ghost


def fill_tables(masked, weight, tables, base):
    high, low = halves(masked)
    result = dot(weight, jnp.concatenate([high, low], axis=0))
    for b in range(CELLS):
        for k in range(RAD):
            tables[base + b, :, k * BLK : (k + 1) * BLK] = block_lanes(
                result[k * F : (k + 1) * F], b
            ).astype(bf16)


def fill_transposed(masked, turned, base):
    high = masked.astype(bf16).astype(f32)
    stacked = jnp.concatenate([high, masked - high], axis=0)
    for b in range(CELLS):
        turned[base + b] = block_lanes(stacked, b).T.astype(bf16)


def fill_columns(small, shift, columns, base):
    third = lax.broadcasted_iota(jnp.int32, (PLACES, BLK), 0) >= 2 * CELLS
    places = small[0:PLACES, :] + jnp.where(third, shift, 0.0)
    turned = jnp.concatenate([places, jnp.zeros((BLK - PLACES, BLK), f32)], axis=0).T
    for b in range(CELLS):
        for c in range(3):
            n = CELLS * c + b
            columns[base + b, c] = jnp.broadcast_to(turned[:, n : n + 1], (BLK, BLK))


def fill_penalty(penalty):
    same = lax.broadcasted_iota(jnp.int32, (BLK, BLK), 0) == lax.broadcasted_iota(
        jnp.int32, (BLK, BLK), 1
    )
    penalty[0] = jnp.zeros((BLK, BLK), f32)
    penalty[1] = jnp.where(same, FAR, 0.0)


def inverse_widths(radial_width):
    return [1.0 / (radial_width[k] * radial_width[k]) for k in range(RAD)]


def decode(pair_list, p):
    code = pair_list[p]
    return lax.shift_right_logical(code, 4), lax.bitwise_and(code, 15)


def separation(rows, columns, penalty, i, j, place):
    parts = [rows[i & 7, c : c + 1, :] - columns[j, c, place, :] for c in range(3)]
    squared = parts[0] * parts[0] + parts[1] * parts[1] + parts[2] * parts[2]
    if penalty is not None:
        squared = squared + penalty[(i == j).astype(jnp.int32), place, :]
    remain = jnp.maximum(1.0 - squared * (1.0 / CUTOFF_SQUARE), 0.0)
    return parts, squared, remain


def message_pass(pair_list, count, rows, columns, penalty, rates, tables, amps, message):
    def amplitudes(p, amp):
        i, j = decode(pair_list, p)
        for r in range(BLK // CHUNK):
            place = slice(r * CHUNK, (r + 1) * CHUNK)
            _, squared, remain = separation(rows, columns, penalty, i, j, place)
            cutoff = remain * remain
            for k in range(RAD):
                value = jnp.exp2(squared * rates[k]) * cutoff
                amp[k * BLK + r * CHUNK : k * BLK + (r + 1) * CHUNK, :] = value.astype(bf16)

    def multiply(p, amp):
        i, j = decode(pair_list, p)
        message[i] += dot(tables[j], amp[...])

    @pl.when(count > 0)
    def _():
        for u, amp in enumerate(amps):
            amplitudes(u, amp)

    def step(t, carry):
        for u, amp in enumerate(amps):
            multiply(GROUP * t + u, amp)
        for u, amp in enumerate(amps):
            amplitudes(GROUP * t + GROUP + u, amp)
        return carry

    lax.fori_loop(0, (count + GROUP - 1) // GROUP, step, 0)


def force_pass(
    pair_list, count, rows, columns, penalty, rates, doubled, turned, down, grads, row_sum, column_sum
):
    lane = lax.broadcasted_iota(jnp.int32, (CHUNK, BLK), 1)

    def products(p, grad):
        i, j = decode(pair_list, p)
        right = down[i]
        grad[...] = dot(turned[j], jnp.concatenate([right, right], axis=0))

    def apply(p, grad):
        i, j = decode(pair_list, p)
        marks = [lane == 3 * j + c for c in range(3)]
        sums = [jnp.zeros((CHUNK, BLK), f32) for _ in range(3)]
        for r in range(BLK // CHUNK):
            place = slice(r * CHUNK, (r + 1) * CHUNK)
            parts, squared, remain = separation(rows, columns, penalty, i, j, place)
            plain = None
            scaled = None
            for k in range(RAD):
                term = jnp.exp2(squared * rates[k]) * grad[place, k * BLK : (k + 1) * BLK]
                plain = term if plain is None else plain + term
                term = term * doubled[k]
                scaled = term if scaled is None else scaled + term
            weighted = remain * (plain + remain * scaled)
            pulls = [weighted * part for part in parts]
            sums = [s + pull for s, pull in zip(sums, pulls)]
            totals = [jnp.sum(pull, axis=1, keepdims=True) for pull in pulls]
            placed = jnp.where(
                marks[0],
                totals[0],
                jnp.where(marks[1], totals[1], jnp.where(marks[2], totals[2], 0.0)),
            )
            column_sum[place, :] += placed
        for c in range(3):
            row_sum[i, c] += sums[c]

    pairs_each = GROUP // 2
    first, second = grads[:pairs_each], grads[pairs_each:]

    @pl.when(count > 0)
    def _():
        for u, grad in enumerate(first):
            products(u, grad)

    def step(t, carry):
        base = GROUP * t
        for u, grad in enumerate(second):
            products(base + pairs_each + u, grad)
        for u, grad in enumerate(first):
            apply(base + u, grad)
        for u, grad in enumerate(first):
            products(base + GROUP + u, grad)
        for u, grad in enumerate(second):
            apply(base + pairs_each + u, grad)
        return carry

    lax.fori_loop(0, (count + GROUP - 1) // GROUP, step, 0)


def own_message_kernel(
    features,
    small,
    small_below,
    small_above,
    pairs,
    npairs,
    radial_width,
    weight,
    out_weight,
    message,
    own_list,
    ghost_list,
    tallies,
    rows,
    columns,
    ghost_columns,
    penalty,
    turned,
    out_column,
    tables,
    *amps,
):
    split_lists(pairs, npairs, own_list, ghost_list, tallies)
    for b in range(CELLS):
        for c in range(3):
            n = CELLS * c + b
            rows[b, c : c + 1, :] = small[n : n + 1, :]
        rows[b, 3:8, :] = jnp.zeros((5, BLK), f32)
    masked = features[...] * occupancy(small)
    fill_tables(masked, jnp.concatenate([weight[...], weight[...]], axis=1), tables, 0)
    fill_transposed(masked, turned, 0)
    fill_columns(small, 0.0, columns, 0)
    fill_columns(small_below, -CELL_SIDE, ghost_columns, 0)
    fill_columns(small_above, CELL_SIDE, ghost_columns, CELLS)
    fill_penalty(penalty)
    out_column[...] = jnp.broadcast_to(as_column(out_weight[...].astype(f32)), (F, BLK))
    message[...] = jnp.zeros(message.shape, f32)
    rates = [-LOG2E * inverse for inverse in inverse_widths(radial_width)]
    message_pass(own_list, tallies[0], rows, columns, penalty, rates, tables, amps, message)


def as_column(row):
    size = (row.shape[1], row.shape[1])
    diagonal = lax.broadcasted_iota(jnp.int32, size, 0) == lax.broadcasted_iota(jnp.int32, size, 1)
    return jnp.sum(jnp.where(diagonal, row, 0.0), axis=1, keepdims=True)


def node_backward(
    message, masked, occupied, weight, update_weight, mix_weight, out_column, down
):
    whole = jnp.concatenate([message[b] for b in range(CELLS)], axis=1)
    scaled = (whole * MESSAGE_SCALE).astype(bf16)
    first_pre = dot(update_weight[...], scaled)
    first_gate = jax.nn.sigmoid(first_pre)
    updated = (masked + first_pre * first_gate).astype(bf16)
    second_pre = dot(mix_weight[...], updated)
    second_gate = jax.nn.sigmoid(second_pre)
    second_grad = (
        jnp.concatenate([out_column[...]] * CELLS, axis=1)
        * second_gate
        * (1.0 + second_pre * (1.0 - second_gate))
        * occupied
    ).astype(bf16)
    update_grad = dot(mix_weight[...], second_grad, ((0,), (0,)))
    first_grad = (update_grad * first_gate * (1.0 + first_pre * (1.0 - first_gate))).astype(bf16)
    downstream = (MESSAGE_SCALE * dot(update_weight[...], first_grad, ((0,), (0,)))).astype(bf16)
    for k in range(RAD):
        mixed = dot(weight[k * F : (k + 1) * F, :], downstream, ((0,), (0,)))
        mixed = (mixed * (4.0 / CUTOFF_SQUARE)).astype(bf16)
        for b in range(CELLS):
            down[b, :, k * BLK : (k + 1) * BLK] = block_lanes(mixed, b)
    down[CELLS] = jnp.zeros((F, RAD * BLK), bf16)


def doubled_rates(inverse):
    return [value * (0.5 * CUTOFF_SQUARE) for value in inverse]


def collect_rows(row_sum, out, start=None):
    for b in range(CELLS):
        for c in range(3):
            total = jnp.sum(row_sum[b, c], axis=0, keepdims=True)
            n = CELLS * c + b
            m = 3 * b + c
            out[n : n + 1, :] = total if start is None else total - start[m : m + 1, :]


def ghost_kernel(
    features,
    small,
    below,
    above,
    small_below,
    small_above,
    own_message,
    rows,
    columns,
    ghost_list,
    tallies,
    radial_width,
    weight,
    update_weight,
    mix_weight,
    out_column,
    row_force,
    ghost_below,
    ghost_above,
    down,
    message,
    tables,
    turned,
    row_sum,
    column_sum,
    *buffers,
):
    amps, grads = buffers[:GROUP], buffers[GROUP:]
    doubled_weight = jnp.concatenate([weight[...], weight[...]], axis=1)
    masked_below = below[...] * occupancy(small_below)
    masked_above = above[...] * occupancy(small_above)
    fill_tables(masked_below, doubled_weight, tables, 0)
    fill_tables(masked_above, doubled_weight, tables, CELLS)
    message[...] = own_message[...]
    inverse = inverse_widths(radial_width)
    rates = [-LOG2E * value for value in inverse]
    count = tallies[1]
    message_pass(ghost_list, count, rows, columns, None, rates, tables, amps, message)
    fill_transposed(below[...] * occupancy(small_below), turned, 0)
    fill_transposed(above[...] * occupancy(small_above), turned, CELLS)
    occupied = occupancy(small)
    node_backward(
        message,
        features[...] * occupied,
        occupied,
        weight,
        update_weight,
        mix_weight,
        out_column,
        down,
    )
    row_sum[...] = jnp.zeros(row_sum.shape, f32)
    column_sum[...] = jnp.zeros(column_sum.shape, f32)
    force_pass(
        ghost_list,
        count,
        rows,
        columns,
        None,
        rates,
        doubled_rates(inverse),
        turned,
        down,
        grads,
        row_sum,
        column_sum,
    )
    collect_rows(row_sum, row_force)
    flat = column_sum[...].T
    ghost_below[...] = flat[0:24]
    ghost_above[...] = flat[24:48]


def own_force_kernel(
    rows,
    columns,
    penalty,
    turned,
    row_force,
    down,
    own_list,
    tallies,
    radial_width,
    force,
    row_sum,
    column_sum,
    *grads,
):
    row_sum[...] = jnp.zeros(row_sum.shape, f32)
    column_sum[...] = jnp.zeros(column_sum.shape, f32)
    inverse = inverse_widths(radial_width)
    rates = [-LOG2E * value for value in inverse]
    force_pass(
        own_list,
        tallies[0],
        rows,
        columns,
        penalty,
        rates,
        doubled_rates(inverse),
        turned,
        down,
        grads,
        row_sum,
        column_sum,
    )
    collect_rows(row_sum, force, column_sum[...].T)
    force[...] += row_force[...]


def by_component(flat):
    return jnp.concatenate(
        [flat[3 * b + c : 3 * b + c + 1, :] for c in range(3) for b in range(CELLS)], axis=0
    )


def finish_kernel(
    force,
    from_above,
    from_below,
    small,
    momenta,
    masses,
    before,
    after,
    leaving,
    forces,
    positions_new,
    momenta_new,
    upward,
    downward,
    packet,
):
    physical = force[...] - by_component(from_above[...] + from_below[...])
    mass = jnp.concatenate([masses[...]] * 3, axis=0)
    current = small[0:PLACES, :]
    spring = -SPRING_RATE * mass * (2.0 * current - before[...] - after[...])
    total = physical + spring
    moved = momenta[...] + total
    placed = current + moved / mass
    forces[...] = total
    momenta_new[...] = moved
    positions_new[...] = placed
    packet[0:24, :] = placed
    packet[24:48, :] = moved
    packet[48:64, :] = jnp.zeros((16, BLK), f32)
    movers = jnp.concatenate([leaving[1:2, :], leaving[0:1, :]], axis=1)
    slot = lax.broadcasted_iota(jnp.int32, (ATOMS_DEV, 2 * MIG), 0)
    chosen = (slot == movers).astype(f32).astype(bf16)
    values = jnp.concatenate([packet[pl.ds(b, 8, stride=CELLS), :] for b in range(CELLS)], axis=1)
    high = values.astype(bf16)
    middle, low = halves(values - high.astype(f32))
    picked = dot(high, chosen) + (dot(middle, chosen) + dot(low, chosen))
    lane = lax.broadcasted_iota(jnp.int32, (8, 2 * MIG), 1)
    row = lax.broadcasted_iota(jnp.int32, (8, 2 * MIG), 0)
    shift = jnp.where(lane < MIG, -CELL_SIDE, CELL_SIDE)
    shifted = jnp.where(movers >= 0, picked + jnp.where(row == 2, shift, 0.0), 0.0)
    up = jnp.where(lane < MIG, shifted, 0.0)
    down = jnp.where(lane < MIG, 0.0, shifted)
    for q in range(6):
        upward[q] = up[q : q + 1, :]
        downward[q] = down[q : q + 1, :]


def effort(microseconds):
    return pl.CostEstimate(
        flops=int(microseconds * 1.0e9),
        transcendentals=0,
        bytes_accessed=int(microseconds * 3.0e6),
    )


def shape(dims, kind=f32):
    return jax.ShapeDtypeStruct(dims, kind)


def body(
    positions,
    momenta,
    features,
    masses,
    radial_width,
    msg_weight,
    update_weight,
    mix_weight,
    out_weight,
    counts,
    pairs,
    npairs,
    leaving,
):
    def ring(axis, step):
        count = lax.axis_size(axis)
        return [(i, (i + step) % count) for i in range(count)]

    up = ring("dom", 1)
    down_ring = ring("dom", -1)
    below = lax.ppermute(features, "dom", up)
    above = lax.ppermute(features, "dom", down_ring)
    weight = msg_weight.reshape(RAD * F, F)
    current = positions.reshape(PLACES, BLK)
    small = pl.pallas_call(
        pack_kernel,
        out_shape=shape((SMALL, BLK)),
        in_specs=[VMEM, SMEM],
        out_specs=VMEM,
        compiler_params=PARAMS,
        cost_estimate=effort(5),
    )(current, counts)
    small_below = lax.ppermute(small, "dom", up)
    small_above = lax.ppermute(small, "dom", down_ring)
    before = lax.ppermute(current, "bead", ring("bead", 1))
    after = lax.ppermute(current, "bead", ring("bead", -1))

    amp = pltpu.VMEM((RAD * BLK, BLK), bf16)
    grad = pltpu.VMEM((BLK, RAD * BLK), f32)
    row_sum = pltpu.VMEM((CELLS + 1, 3, CHUNK, BLK), f32)
    column_sum = pltpu.VMEM((BLK, BLK), f32)
    listed = shape((pairs.shape[1] + 8,), jnp.int32)

    def tables(blocks):
        return pltpu.VMEM((blocks, F, RAD * BLK), bf16)

    (
        own_message,
        own_list,
        ghost_list,
        tallies,
        rows,
        columns,
        ghost_columns,
        penalty,
        turned,
        out_column,
    ) = pl.pallas_call(
        own_message_kernel,
        out_shape=(
            shape((CELLS + 1, F, BLK)),
            listed,
            listed,
            shape((2,), jnp.int32),
            shape((CELLS, 8, BLK)),
            shape((CELLS, 3, BLK, BLK)),
            shape((2 * CELLS, 3, BLK, BLK)),
            shape((2, BLK, BLK)),
            shape((CELLS, BLK, BLK), bf16),
            shape((F, BLK)),
        ),
        in_specs=[VMEM] * 4 + [SMEM] * 3 + [VMEM] * 2,
        out_specs=(VMEM, SMEM, SMEM, SMEM) + (VMEM,) * 6,
        scratch_shapes=[tables(CELLS)] + [amp] * GROUP,
        compiler_params=PARAMS,
    )(
        features,
        small,
        small_below,
        small_above,
        pairs,
        npairs,
        radial_width,
        weight,
        out_weight.reshape(1, F),
    )
    row_force, ghost_below, ghost_above, down = pl.pallas_call(
        ghost_kernel,
        out_shape=(
            shape((PLACES, BLK)),
            shape((PLACES, BLK)),
            shape((PLACES, BLK)),
            shape((CELLS + 1, F, RAD * BLK), bf16),
        ),
        in_specs=[VMEM] * 9 + [SMEM] * 3 + [VMEM] * 4,
        out_specs=(VMEM,) * 4,
        scratch_shapes=[
            pltpu.VMEM((CELLS + 1, F, BLK), f32),
            tables(2 * CELLS),
            pltpu.VMEM((2 * CELLS, BLK, BLK), bf16),
            row_sum,
            column_sum,
        ]
        + [amp] * GROUP
        + [grad] * GROUP,
        compiler_params=PARAMS,
    )(
        features,
        small,
        below,
        above,
        small_below,
        small_above,
        own_message,
        rows,
        ghost_columns,
        ghost_list,
        tallies,
        radial_width,
        weight,
        update_weight,
        mix_weight,
        out_column,
    )
    from_above = lax.ppermute(ghost_below, "dom", down_ring)
    from_below = lax.ppermute(ghost_above, "dom", up)
    force = pl.pallas_call(
        own_force_kernel,
        out_shape=shape((PLACES, BLK)),
        in_specs=[VMEM] * 6 + [SMEM] * 3,
        out_specs=VMEM,
        scratch_shapes=[row_sum, column_sum] + [grad] * GROUP,
        compiler_params=PARAMS,
    )(rows, columns, penalty, turned, row_force, down, own_list, tallies, radial_width)
    whole = shape((PLACES, BLK))
    packet = shape((6, 1, 2 * MIG))
    forces, positions_new, momenta_new, upward, downward = pl.pallas_call(
        finish_kernel,
        out_shape=(whole, whole, whole, packet, packet),
        in_specs=[VMEM] * 9,
        out_specs=(VMEM,) * 5,
        scratch_shapes=[pltpu.VMEM((64, BLK), f32)],
        compiler_params=PARAMS,
    )(
        force,
        from_above,
        from_below,
        small,
        momenta.reshape(PLACES, BLK),
        masses.reshape(CELLS, BLK),
        before,
        after,
        leaving,
    )
    arrivals = lax.ppermute(upward, "dom", up) + lax.ppermute(downward, "dom", down_ring)
    result = tuple(x.reshape(1, 3, ATOMS_DEV) for x in (forces, positions_new, momenta_new))
    return result + (arrivals.reshape(1, 6, 2 * MIG),)


def solution(mesh):
    split = P("bead", None, "dom")
    in_specs = (
        split,
        split,
        P(None, "dom"),
        P("dom"),
        P(),
        P(),
        P(),
        P(),
        P(),
        P("dom"),
        P(None, "dom"),
        P("dom"),
        P(None, "dom"),
    )
    out_specs = (split, split, split, split)
    return jax.shard_map(body, mesh=mesh, in_specs=in_specs, out_specs=out_specs, check_vma=False)
```

```python
from functools import partial

import jax
import jax.numpy as jnp
from jax import lax
from jax.experimental import pallas as pl
from jax.experimental.pallas import tpu as pltpu
from jax.sharding import PartitionSpec as P

F = 64
RAD = 4
BLK = 128
MIG = 64
CELLS = 8
ATOMS_DEV = CELLS * BLK
PLACES = 3 * CELLS
SMALL = PLACES + CELLS

CUTOFF_SQUARE = 36.0
CELL_SIDE = 10.0
MESSAGE_SCALE = 0.25
SPRING_RATE = 0.2
LOG2E = 1.4426950408889634
FAR = 1.0e9
CHUNK = 16
GROUP = 4

f32 = jnp.float32
bf16 = jnp.bfloat16
VMEM = pl.BlockSpec(memory_space=pltpu.VMEM)
SMEM = pl.BlockSpec(memory_space=pltpu.SMEM)
PARAMS = pltpu.CompilerParams(vmem_limit_bytes=48 * 1024 * 1024)


def dot(a, b, dims=((1,), (0,))):
    return lax.dot_general(a, b, (dims, ((), ())), preferred_element_type=f32)


def halves(x):
    high = x.astype(bf16)
    return high, (x - high.astype(f32)).astype(bf16)


def block_lanes(x, b):
    return x[:, b * BLK : (b + 1) * BLK]


def pack_kernel(positions, counts, small):
    lane = lax.broadcasted_iota(jnp.int32, (1, BLK), 1)
    small[0:PLACES, :] = positions[...]
    for b in range(CELLS):
        small[PLACES + b : PLACES + b + 1, :] = (lane < counts[b]).astype(f32)


def occupancy(small):
    return jnp.concatenate([small[PLACES + b : PLACES + b + 1, :] for b in range(CELLS)], axis=1)


def split_lists(pairs, npairs, own_list, ghost_list, tallies):
    def step(p, carry):
        own, ghost = carry
        i = pairs[0, p]
        j = pairs[1, p]
        mine = jnp.logical_and(j >= CELLS, j < 2 * CELLS)
        shifted = jnp.where(mine, j - CELLS, jnp.where(j >= 2 * CELLS, j - CELLS, j))
        code = i * 16 + shifted
        own_list[own] = code
        ghost_list[ghost] = code
        taken = mine.astype(jnp.int32)
        return own + taken, ghost + 1 - taken

    own, ghost = lax.fori_loop(0, npairs[0], step, (jnp.int32(0), jnp.int32(0)))
    for extra in range(2 * GROUP):
        own_list[own + extra] = CELLS * 16
        ghost_list[ghost + extra] = CELLS * 16
    tallies[0] = own
    tallies[1] = ghost


def fill_tables(masked, weight, tables, base):
    high, low = halves(masked)
    result = dot(weight, jnp.concatenate([high, low], axis=0))
    for b in range(CELLS):
        for k in range(RAD):
            tables[base + b, :, k * BLK : (k + 1) * BLK] = block_lanes(
                result[k * F : (k + 1) * F], b
            ).astype(bf16)


def fill_transposed(masked, turned, base):
    high = masked.astype(bf16).astype(f32)
    stacked = jnp.concatenate([high, masked - high], axis=0)
    for b in range(CELLS):
        turned[base + b] = block_lanes(stacked, b).T.astype(bf16)


def fill_columns(small, shift, columns, base):
    third = lax.broadcasted_iota(jnp.int32, (PLACES, BLK), 0) >= 2 * CELLS
    places = small[0:PLACES, :] + jnp.where(third, shift, 0.0)
    turned = jnp.concatenate([places, jnp.zeros((BLK - PLACES, BLK), f32)], axis=0).T
    for b in range(CELLS):
        for c in range(3):
            n = CELLS * c + b
            columns[base + b, c] = jnp.broadcast_to(turned[:, n : n + 1], (BLK, BLK))


def fill_penalty(penalty):
    same = lax.broadcasted_iota(jnp.int32, (BLK, BLK), 0) == lax.broadcasted_iota(
        jnp.int32, (BLK, BLK), 1
    )
    penalty[0] = jnp.zeros((BLK, BLK), f32)
    penalty[1] = jnp.where(same, FAR, 0.0)


def inverse_widths(radial_width):
    return [1.0 / (radial_width[k] * radial_width[k]) for k in range(RAD)]


def decode(pair_list, p):
    code = pair_list[p]
    return lax.shift_right_logical(code, 4), lax.bitwise_and(code, 15)


def separation(rows, columns, penalty, i, j, place):
    parts = [rows[i & 7, c : c + 1, :] - columns[j, c, place, :] for c in range(3)]
    squared = parts[0] * parts[0] + parts[1] * parts[1] + parts[2] * parts[2]
    if penalty is not None:
        squared = squared + penalty[(i == j).astype(jnp.int32), place, :]
    remain = jnp.maximum(1.0 - squared * (1.0 / CUTOFF_SQUARE), 0.0)
    return parts, squared, remain


def message_pass(pair_list, count, rows, columns, penalty, rates, tables, amps, message):
    def amplitudes(p, amp):
        i, j = decode(pair_list, p)
        for r in range(BLK // CHUNK):
            place = slice(r * CHUNK, (r + 1) * CHUNK)
            _, squared, remain = separation(rows, columns, penalty, i, j, place)
            cutoff = remain * remain
            for k in range(RAD):
                value = jnp.exp2(squared * rates[k]) * cutoff
                amp[k * BLK + r * CHUNK : k * BLK + (r + 1) * CHUNK, :] = value.astype(bf16)

    def multiply(p, amp):
        i, j = decode(pair_list, p)
        message[i] += dot(tables[j], amp[...])

    @pl.when(count > 0)
    def _():
        for u, amp in enumerate(amps):
            amplitudes(u, amp)

    def step(t, carry):
        for u, amp in enumerate(amps):
            multiply(GROUP * t + u, amp)
        for u, amp in enumerate(amps):
            amplitudes(GROUP * t + GROUP + u, amp)
        return carry

    lax.fori_loop(0, (count + GROUP - 1) // GROUP, step, 0)


def force_pass(
    pair_list, count, rows, columns, penalty, rates, doubled, turned, down, grads, row_sum, column_sum
):
    lane = lax.broadcasted_iota(jnp.int32, (CHUNK, BLK), 1)

    def products(p, grad):
        i, j = decode(pair_list, p)
        right = down[i]
        grad[...] = dot(turned[j], jnp.concatenate([right, right], axis=0))

    def apply(p, grad):
        i, j = decode(pair_list, p)
        marks = [lane == 3 * j + c for c in range(3)]
        sums = [jnp.zeros((CHUNK, BLK), f32) for _ in range(3)]
        for r in range(BLK // CHUNK):
            place = slice(r * CHUNK, (r + 1) * CHUNK)
            parts, squared, remain = separation(rows, columns, penalty, i, j, place)
            plain = None
            scaled = None
            for k in range(RAD):
                term = jnp.exp2(squared * rates[k]) * grad[place, k * BLK : (k + 1) * BLK]
                plain = term if plain is None else plain + term
                term = term * doubled[k]
                scaled = term if scaled is None else scaled + term
            weighted = remain * (plain + remain * scaled)
            pulls = [weighted * part for part in parts]
            sums = [s + pull for s, pull in zip(sums, pulls)]
            totals = [jnp.sum(pull, axis=1, keepdims=True) for pull in pulls]
            placed = jnp.where(
                marks[0],
                totals[0],
                jnp.where(marks[1], totals[1], jnp.where(marks[2], totals[2], 0.0)),
            )
            column_sum[place, :] += placed
        for c in range(3):
            row_sum[i, c] += sums[c]

    pairs_each = GROUP // 2
    first, second = grads[:pairs_each], grads[pairs_each:]

    @pl.when(count > 0)
    def _():
        for u, grad in enumerate(first):
            products(u, grad)

    def step(t, carry):
        base = GROUP * t
        for u, grad in enumerate(second):
            products(base + pairs_each + u, grad)
        for u, grad in enumerate(first):
            apply(base + u, grad)
        for u, grad in enumerate(first):
            products(base + GROUP + u, grad)
        for u, grad in enumerate(second):
            apply(base + pairs_each + u, grad)
        return carry

    lax.fori_loop(0, (count + GROUP - 1) // GROUP, step, 0)


def own_message_kernel(
    features,
    small,
    pairs,
    npairs,
    radial_width,
    weight,
    out_weight,
    message,
    own_list,
    ghost_list,
    tallies,
    rows,
    columns,
    penalty,
    turned,
    out_column,
    tables,
    *amps,
):
    split_lists(pairs, npairs, own_list, ghost_list, tallies)
    for b in range(CELLS):
        for c in range(3):
            n = CELLS * c + b
            rows[b, c : c + 1, :] = small[n : n + 1, :]
        rows[b, 3:8, :] = jnp.zeros((5, BLK), f32)
    masked = features[...] * occupancy(small)
    fill_tables(masked, jnp.concatenate([weight[...], weight[...]], axis=1), tables, 0)
    fill_transposed(masked, turned, 0)
    fill_columns(small, 0.0, columns, 0)
    fill_penalty(penalty)
    out_column[...] = jnp.broadcast_to(as_column(out_weight[...].astype(f32)), (F, BLK))
    message[...] = jnp.zeros(message.shape, f32)
    rates = [-LOG2E * inverse for inverse in inverse_widths(radial_width)]
    message_pass(own_list, tallies[0], rows, columns, penalty, rates, tables, amps, message)


def as_column(row):
    size = (row.shape[1], row.shape[1])
    diagonal = lax.broadcasted_iota(jnp.int32, size, 0) == lax.broadcasted_iota(jnp.int32, size, 1)
    return jnp.sum(jnp.where(diagonal, row, 0.0), axis=1, keepdims=True)


def node_backward(
    message, masked, occupied, weight, update_weight, mix_weight, out_column, down
):
    whole = jnp.concatenate([message[b] for b in range(CELLS)], axis=1)
    scaled = (whole * MESSAGE_SCALE).astype(bf16)
    first_pre = dot(update_weight[...], scaled)
    first_gate = jax.nn.sigmoid(first_pre)
    updated = (masked + first_pre * first_gate).astype(bf16)
    second_pre = dot(mix_weight[...], updated)
    second_gate = jax.nn.sigmoid(second_pre)
    second_grad = (
        jnp.concatenate([out_column[...]] * CELLS, axis=1)
        * second_gate
        * (1.0 + second_pre * (1.0 - second_gate))
        * occupied
    ).astype(bf16)
    update_grad = dot(mix_weight[...], second_grad, ((0,), (0,)))
    first_grad = (update_grad * first_gate * (1.0 + first_pre * (1.0 - first_gate))).astype(bf16)
    downstream = (MESSAGE_SCALE * dot(update_weight[...], first_grad, ((0,), (0,)))).astype(bf16)
    for k in range(RAD):
        mixed = dot(weight[k * F : (k + 1) * F, :], downstream, ((0,), (0,)))
        mixed = (mixed * (4.0 / CUTOFF_SQUARE)).astype(bf16)
        for b in range(CELLS):
            down[b, :, k * BLK : (k + 1) * BLK] = block_lanes(mixed, b)
    down[CELLS] = jnp.zeros((F, RAD * BLK), bf16)


def doubled_rates(inverse):
    return [value * (0.5 * CUTOFF_SQUARE) for value in inverse]


def collect_rows(row_sum, out, start=None):
    for b in range(CELLS):
        for c in range(3):
            total = jnp.sum(row_sum[b, c], axis=0, keepdims=True)
            n = CELLS * c + b
            m = 3 * b + c
            out[n : n + 1, :] = total if start is None else total - start[m : m + 1, :]


def ghost_kernel(
    features,
    small,
    below,
    above,
    small_below,
    small_above,
    own_message,
    rows,
    ghost_list,
    tallies,
    radial_width,
    weight,
    update_weight,
    mix_weight,
    out_column,
    row_force,
    ghost_below,
    ghost_above,
    down,
    message,
    tables,
    turned,
    columns,
    row_sum,
    column_sum,
    *buffers,
):
    amps, grads = buffers[:GROUP], buffers[GROUP:]
    fill_columns(small_below, -CELL_SIDE, columns, 0)
    fill_columns(small_above, CELL_SIDE, columns, CELLS)
    doubled_weight = jnp.concatenate([weight[...], weight[...]], axis=1)
    masked_below = below[...] * occupancy(small_below)
    masked_above = above[...] * occupancy(small_above)
    fill_tables(masked_below, doubled_weight, tables, 0)
    fill_tables(masked_above, doubled_weight, tables, CELLS)
    message[...] = own_message[...]
    inverse = inverse_widths(radial_width)
    rates = [-LOG2E * value for value in inverse]
    count = tallies[1]
    message_pass(ghost_list, count, rows, columns, None, rates, tables, amps, message)
    fill_transposed(below[...] * occupancy(small_below), turned, 0)
    fill_transposed(above[...] * occupancy(small_above), turned, CELLS)
    occupied = occupancy(small)
    node_backward(
        message,
        features[...] * occupied,
        occupied,
        weight,
        update_weight,
        mix_weight,
        out_column,
        down,
    )
    row_sum[...] = jnp.zeros(row_sum.shape, f32)
    column_sum[...] = jnp.zeros(column_sum.shape, f32)
    force_pass(
        ghost_list,
        count,
        rows,
        columns,
        None,
        rates,
        doubled_rates(inverse),
        turned,
        down,
        grads,
        row_sum,
        column_sum,
    )
    collect_rows(row_sum, row_force)
    flat = column_sum[...].T
    ghost_below[...] = flat[0:24]
    ghost_above[...] = flat[24:48]


def own_force_kernel(
    rows,
    columns,
    penalty,
    turned,
    row_force,
    down,
    own_list,
    tallies,
    radial_width,
    force,
    row_sum,
    column_sum,
    *grads,
):
    row_sum[...] = jnp.zeros(row_sum.shape, f32)
    column_sum[...] = jnp.zeros(column_sum.shape, f32)
    inverse = inverse_widths(radial_width)
    rates = [-LOG2E * value for value in inverse]
    force_pass(
        own_list,
        tallies[0],
        rows,
        columns,
        penalty,
        rates,
        doubled_rates(inverse),
        turned,
        down,
        grads,
        row_sum,
        column_sum,
    )
    collect_rows(row_sum, force, column_sum[...].T)
    force[...] += row_force[...]


def by_component(flat):
    return jnp.concatenate(
        [flat[3 * b + c : 3 * b + c + 1, :] for c in range(3) for b in range(CELLS)], axis=0
    )


def finish_kernel(
    force,
    from_above,
    from_below,
    small,
    momenta,
    masses,
    before,
    after,
    leaving,
    forces,
    positions_new,
    momenta_new,
    upward,
    downward,
    packet,
):
    physical = force[...] - by_component(from_above[...] + from_below[...])
    mass = jnp.concatenate([masses[...]] * 3, axis=0)
    current = small[0:PLACES, :]
    spring = -SPRING_RATE * mass * (2.0 * current - before[...] - after[...])
    total = physical + spring
    moved = momenta[...] + total
    placed = current + moved / mass
    forces[...] = total
    momenta_new[...] = moved
    positions_new[...] = placed
    packet[0:24, :] = placed
    packet[24:48, :] = moved
    packet[48:64, :] = jnp.zeros((16, BLK), f32)
    movers = jnp.concatenate([leaving[1:2, :], leaving[0:1, :]], axis=1)
    slot = lax.broadcasted_iota(jnp.int32, (ATOMS_DEV, 2 * MIG), 0)
    chosen = (slot == movers).astype(f32).astype(bf16)
    values = jnp.concatenate([packet[pl.ds(b, 8, stride=CELLS), :] for b in range(CELLS)], axis=1)
    high = values.astype(bf16)
    middle, low = halves(values - high.astype(f32))
    picked = dot(high, chosen) + (dot(middle, chosen) + dot(low, chosen))
    lane = lax.broadcasted_iota(jnp.int32, (8, 2 * MIG), 1)
    row = lax.broadcasted_iota(jnp.int32, (8, 2 * MIG), 0)
    shift = jnp.where(lane < MIG, -CELL_SIDE, CELL_SIDE)
    shifted = jnp.where(movers >= 0, picked + jnp.where(row == 2, shift, 0.0), 0.0)
    up = jnp.where(lane < MIG, shifted, 0.0)
    down = jnp.where(lane < MIG, 0.0, shifted)
    for q in range(6):
        upward[q] = up[q : q + 1, :]
        downward[q] = down[q : q + 1, :]


def effort(microseconds):
    return pl.CostEstimate(
        flops=int(microseconds * 1.0e9),
        transcendentals=0,
        bytes_accessed=int(microseconds * 3.0e6),
    )


def shape(dims, kind=f32):
    return jax.ShapeDtypeStruct(dims, kind)


def body(
    positions,
    momenta,
    features,
    masses,
    radial_width,
    msg_weight,
    update_weight,
    mix_weight,
    out_weight,
    counts,
    pairs,
    npairs,
    leaving,
):
    def ring(axis, step):
        count = lax.axis_size(axis)
        return [(i, (i + step) % count) for i in range(count)]

    up = ring("dom", 1)
    down_ring = ring("dom", -1)
    below = lax.ppermute(features, "dom", up)
    above = lax.ppermute(features, "dom", down_ring)
    weight = msg_weight.reshape(RAD * F, F)
    current = positions.reshape(PLACES, BLK)
    small = pl.pallas_call(
        pack_kernel,
        out_shape=shape((SMALL, BLK)),
        in_specs=[VMEM, SMEM],
        out_specs=VMEM,
        compiler_params=PARAMS,
        cost_estimate=effort(5),
    )(current, counts)
    small_below = lax.ppermute(small, "dom", up)
    small_above = lax.ppermute(small, "dom", down_ring)

    amp = pltpu.VMEM((RAD * BLK, BLK), bf16)
    grad = pltpu.VMEM((BLK, RAD * BLK), f32)
    row_sum = pltpu.VMEM((CELLS + 1, 3, CHUNK, BLK), f32)
    column_sum = pltpu.VMEM((BLK, BLK), f32)
    listed = shape((pairs.shape[1] + 8,), jnp.int32)

    def tables(blocks):
        return pltpu.VMEM((blocks, F, RAD * BLK), bf16)

    (
        own_message,
        own_list,
        ghost_list,
        tallies,
        rows,
        columns,
        penalty,
        turned,
        out_column,
    ) = pl.pallas_call(
        own_message_kernel,
        out_shape=(
            shape((CELLS + 1, F, BLK)),
            listed,
            listed,
            shape((2,), jnp.int32),
            shape((CELLS, 8, BLK)),
            shape((CELLS, 3, BLK, BLK)),
            shape((2, BLK, BLK)),
            shape((CELLS, BLK, BLK), bf16),
            shape((F, BLK)),
        ),
        in_specs=[VMEM] * 2 + [SMEM] * 3 + [VMEM] * 2,
        out_specs=(VMEM, SMEM, SMEM, SMEM) + (VMEM,) * 5,
        scratch_shapes=[tables(CELLS)] + [amp] * GROUP,
        compiler_params=PARAMS,
    )(
        features,
        small,
        pairs,
        npairs,
        radial_width,
        weight,
        out_weight.reshape(1, F),
    )
    late, own_message = lax.optimization_barrier((current, own_message))
    before = lax.ppermute(late, "bead", ring("bead", 1))
    after = lax.ppermute(late, "bead", ring("bead", -1))
    row_force, ghost_below, ghost_above, down = pl.pallas_call(
        ghost_kernel,
        out_shape=(
            shape((PLACES, BLK)),
            shape((PLACES, BLK)),
            shape((PLACES, BLK)),
            shape((CELLS + 1, F, RAD * BLK), bf16),
        ),
        in_specs=[VMEM] * 8 + [SMEM] * 3 + [VMEM] * 4,
        out_specs=(VMEM,) * 4,
        scratch_shapes=[
            pltpu.VMEM((CELLS + 1, F, BLK), f32),
            tables(2 * CELLS),
            pltpu.VMEM((2 * CELLS, BLK, BLK), bf16),
            pltpu.VMEM((2 * CELLS, 3, BLK, BLK), f32),
            row_sum,
            column_sum,
        ]
        + [amp] * GROUP
        + [grad] * GROUP,
        compiler_params=PARAMS,
    )(
        features,
        small,
        below,
        above,
        small_below,
        small_above,
        own_message,
        rows,
        ghost_list,
        tallies,
        radial_width,
        weight,
        update_weight,
        mix_weight,
        out_column,
    )
    from_above = lax.ppermute(ghost_below, "dom", down_ring)
    from_below = lax.ppermute(ghost_above, "dom", up)
    force = pl.pallas_call(
        own_force_kernel,
        out_shape=shape((PLACES, BLK)),
        in_specs=[VMEM] * 6 + [SMEM] * 3,
        out_specs=VMEM,
        scratch_shapes=[row_sum, column_sum] + [grad] * GROUP,
        compiler_params=PARAMS,
    )(rows, columns, penalty, turned, row_force, down, own_list, tallies, radial_width)
    whole = shape((PLACES, BLK))
    packet = shape((6, 1, 2 * MIG))
    forces, positions_new, momenta_new, upward, downward = pl.pallas_call(
        finish_kernel,
        out_shape=(whole, whole, whole, packet, packet),
        in_specs=[VMEM] * 9,
        out_specs=(VMEM,) * 5,
        scratch_shapes=[pltpu.VMEM((64, BLK), f32)],
        compiler_params=PARAMS,
    )(
        force,
        from_above,
        from_below,
        small,
        momenta.reshape(PLACES, BLK),
        masses.reshape(CELLS, BLK),
        before,
        after,
        leaving,
    )
    arrivals = lax.ppermute(upward, "dom", up) + lax.ppermute(downward, "dom", down_ring)
    result = tuple(x.reshape(1, 3, ATOMS_DEV) for x in (forces, positions_new, momenta_new))
    return result + (arrivals.reshape(1, 6, 2 * MIG),)


def solution(mesh):
    split = P("bead", None, "dom")
    in_specs = (
        split,
        split,
        P(None, "dom"),
        P("dom"),
        P(),
        P(),
        P(),
        P(),
        P(),
        P("dom"),
        P(None, "dom"),
        P("dom"),
        P(None, "dom"),
    )
    out_specs = (split, split, split, split)
    return jax.shard_map(body, mesh=mesh, in_specs=in_specs, out_specs=out_specs, check_vma=False)
```

```python
from functools import partial

import jax
import jax.numpy as jnp
from jax import lax
from jax.experimental import pallas as pl
from jax.experimental.pallas import tpu as pltpu
from jax.sharding import PartitionSpec as P

F = 64
RAD = 4
BLK = 128
MIG = 64
CELLS = 8
ATOMS_DEV = CELLS * BLK
PLACES = 3 * CELLS
SMALL = PLACES + CELLS

CUTOFF = 6.0
CUTOFF_SQUARE = CUTOFF * CUTOFF
CELL_SIDE = 10.0
MESSAGE_SCALE = 0.25
SPRING_RATE = 0.2
LOG2E = 1.4426950408889634
FAR = 1.0e9
REACH = 1.001
FEWER = 96
CHUNK = 16
GROUP = 8
BATCH = 8

f32 = jnp.float32
bf16 = jnp.bfloat16
VMEM = pl.BlockSpec(memory_space=pltpu.VMEM)
SMEM = pl.BlockSpec(memory_space=pltpu.SMEM)
PARAMS = pltpu.CompilerParams(vmem_limit_bytes=32 * 1024 * 1024)


def dot(a, b, dims=((1,), (0,))):
    return lax.dot_general(a, b, (dims, ((), ())), preferred_element_type=f32)


def halves(x):
    high = x.astype(bf16)
    return high, (x - high.astype(f32)).astype(bf16)


def block_lanes(x, b):
    return x[:, b * BLK : (b + 1) * BLK]


def pack_kernel(positions, counts, small):
    lane = lax.broadcasted_iota(jnp.int32, (1, BLK), 1)
    small[0:PLACES, :] = positions[...]
    for b in range(CELLS):
        small[PLACES + b : PLACES + b + 1, :] = (lane < counts[b]).astype(f32)


def occupancy(small):
    return jnp.concatenate([small[PLACES + b : PLACES + b + 1, :] for b in range(CELLS)], axis=1)


def split_lists(pairs, npairs, own_list, ghost_list, tallies):
    def step(p, carry):
        own, ghost = carry
        i = pairs[0, p]
        j = pairs[1, p]
        mine = jnp.logical_and(j >= CELLS, j < 2 * CELLS)
        shifted = jnp.where(mine, j - CELLS, jnp.where(j >= 2 * CELLS, j - CELLS, j))
        code = i * 16 + shifted
        own_list[own] = code
        ghost_list[ghost] = code
        taken = mine.astype(jnp.int32)
        return own + taken, ghost + 1 - taken

    own, ghost = lax.fori_loop(0, npairs[0], step, (jnp.int32(0), jnp.int32(0)))
    for extra in range(2 * BATCH):
        own_list[own + extra] = CELLS * 16
        ghost_list[ghost + extra] = CELLS * 16
    tallies[0] = own
    tallies[1] = ghost


def fill_tables(masked, weight, tables, base):
    high, low = halves(masked)
    result = dot(weight, jnp.concatenate([high, low], axis=0))
    for b in range(CELLS):
        for k in range(RAD):
            tables[base + b, :, k * BLK : (k + 1) * BLK] = block_lanes(
                result[k * F : (k + 1) * F], b
            ).astype(bf16)


def fill_transposed(masked, turned, base):
    high = masked.astype(bf16).astype(f32)
    stacked = jnp.concatenate([high, masked - high], axis=0)
    for b in range(CELLS):
        turned[base + b] = block_lanes(stacked, b).T.astype(bf16)


def fill_columns(small, shift, columns, base):
    third = lax.broadcasted_iota(jnp.int32, (PLACES, BLK), 0) >= 2 * CELLS
    places = (small[0:PLACES, :] + jnp.where(third, shift, 0.0)) * (1.0 / CUTOFF)
    turned = jnp.concatenate([places, jnp.zeros((BLK - PLACES, BLK), f32)], axis=0).T
    for b in range(CELLS):
        for c in range(3):
            n = CELLS * c + b
            columns[base + b, c] = jnp.broadcast_to(turned[:, n : n + 1], (BLK, BLK))


def near_first(smalls, shifts, small, places):
    pieces = []
    for part, shift in zip(smalls, shifts):
        third = lax.broadcasted_iota(jnp.int32, (PLACES, BLK), 0) >= 2 * CELLS
        moved = (part[0:PLACES, :] + jnp.where(third, shift, 0.0)) * (1.0 / CUTOFF)
        pieces += [moved, part[PLACES:SMALL, :]]
    pieces.append(jnp.zeros((BLK - 2 * SMALL, BLK), f32))
    flat = jnp.concatenate(pieces, axis=0)
    places[...] = flat
    turned = flat.T
    heights = small[2 * CELLS : PLACES, :] * (1.0 / CUTOFF)
    held = small[PLACES:SMALL, :] > 0.5
    lowest = jnp.min(jnp.where(held, heights, FAR))
    highest = jnp.max(jnp.where(held, heights, -FAR))
    inside = jnp.logical_and(turned > lowest - REACH, turned < highest + REACH)
    present = pltpu.roll(turned, BLK - CELLS, 1) > 0.5
    near = jnp.where(jnp.logical_and(inside, present), 1.0, 0.0)
    ahead = lax.broadcasted_iota(jnp.int32, (BLK, BLK), 1) < lax.broadcasted_iota(
        jnp.int32, (BLK, BLK), 0
    )
    rank = dot(jnp.where(ahead, 1.0, 0.0).astype(bf16), near.astype(bf16))
    lane = lax.broadcasted_iota(jnp.int32, (1, BLK), 1)
    height_lane = jnp.bitwise_and(lax.shift_right_logical(lane, 3), 3) == 2
    height_lane = jnp.logical_and(height_lane, lane < 2 * SMALL)
    total = jnp.sum(near, axis=0, keepdims=True)
    most = jnp.max(jnp.where(height_lane, total, 0.0))
    return jnp.where(near > 0.5, rank, -1.0), most


def fill_ghosts(smalls, features, slots, places, weight, chosen, tables, turned, columns):
    lane = lax.broadcasted_iota(jnp.int32, (BLK, BLK), 1).astype(f32)
    for side in range(2):
        masked = features[side][...] * occupancy(smalls[side])
        high = masked.astype(bf16).astype(f32)
        low = masked - high
        for b in range(CELLS):
            n = side * CELLS + b
            place = side * SMALL + 2 * CELLS + b
            slot = jnp.broadcast_to(slots[:, place : place + 1], (BLK, BLK))
            pick = jnp.where(slot == lane, 1.0, 0.0).astype(bf16)
            chosen[n] = pick
            three = [
                places[side * SMALL + CELLS * c + b : side * SMALL + CELLS * c + b + 1, :]
                for c in range(3)
            ]
            here = jnp.concatenate(three + [jnp.zeros((5, BLK), f32)], axis=0)
            first = here.astype(bf16).astype(f32)
            second = (here - first).astype(bf16).astype(f32)
            parts = [block_lanes(high, b), block_lanes(low, b)]
            parts += [first, second, here - first - second]
            moved = dot(jnp.concatenate(parts, axis=0).astype(bf16), pick)
            spots = moved[2 * F : 2 * F + 8] + moved[2 * F + 8 : 2 * F + 16] + moved[2 * F + 16 :]
            for c in range(3):
                columns[n, c] = jnp.broadcast_to(spots[c : c + 1, :], (BLK, BLK)).T
            halved = moved[0 : 2 * F]
            result = dot(weight, halved.astype(bf16))
            for k in range(RAD):
                tables[n, :, k * BLK : (k + 1) * BLK] = result[k * F : (k + 1) * F].astype(bf16)
            turned[n] = halved.T.astype(bf16)


def return_ghosts(column_sum, chosen, outs):
    flat = column_sum[...].T
    for side in range(2):
        for b in range(CELLS):
            n = side * CELLS + b
            piece = jnp.concatenate([flat[3 * n : 3 * n + 3], jnp.zeros((5, BLK), f32)], axis=0)
            first = piece.astype(bf16).astype(f32)
            both = jnp.concatenate([first, piece - first], axis=0).astype(bf16)
            back = dot(both, chosen[n], ((1,), (1,)))
            outs[side][3 * b : 3 * b + 3, :] = back[0:3] + back[8:11]


def fill_penalty(penalty):
    same = lax.broadcasted_iota(jnp.int32, (BLK, BLK), 0) == lax.broadcasted_iota(
        jnp.int32, (BLK, BLK), 1
    )
    penalty[0] = jnp.zeros((BLK, BLK), f32)
    penalty[1] = jnp.where(same, FAR, 0.0)


def inverse_widths(radial_width):
    return [1.0 / (radial_width[k] * radial_width[k]) for k in range(RAD)]


def decay_rates(inverse):
    return [value * (-LOG2E * CUTOFF_SQUARE) for value in inverse]


def decode(pair_list, p):
    code = pair_list[p]
    return lax.shift_right_logical(code, 4), lax.bitwise_and(code, 15)


def separation(rows, columns, penalty, i, j, place):
    parts = [rows[i & 7, c : c + 1, :] - columns[j, c, place, :] for c in range(3)]
    squared = parts[0] * parts[0] + parts[1] * parts[1] + parts[2] * parts[2]
    if penalty is not None:
        squared = squared + penalty[(i == j).astype(jnp.int32), place, :]
    remain = jnp.maximum(1.0 - squared, 0.0)
    return parts, squared, remain


def message_pass(
    pair_list, count, rows, columns, penalty, rates, tables, amps, message, used=BLK
):
    def amplitudes(p, amp):
        i, j = decode(pair_list, p)
        for r in range(used // CHUNK):
            place = slice(r * CHUNK, (r + 1) * CHUNK)
            _, squared, remain = separation(rows, columns, penalty, i, j, place)
            cutoff = remain * remain
            for k in range(RAD):
                decay = jnp.exp2(squared * rates[k])
                value = decay * cutoff
                amp[k * BLK + r * CHUNK : k * BLK + (r + 1) * CHUNK, :] = value.astype(bf16)

    def multiply(p, amp):
        i, j = decode(pair_list, p)
        message[i] += dot(tables[j], amp[...])

    @pl.when(count > 0)
    def _():
        for u, amp in enumerate(amps):
            amplitudes(u, amp)

    def step(t, carry):
        for u, amp in enumerate(amps):
            multiply(BATCH * t + u, amp)
        for u, amp in enumerate(amps):
            amplitudes(BATCH * t + BATCH + u, amp)
        return carry

    lax.fori_loop(0, (count + BATCH - 1) // BATCH, step, 0)


def force_pass(
    pair_list, count, rows, columns, penalty, rates, doubled, turned, down, grads, row_sum, column_sum,
    used=BLK,
):
    lane = lax.broadcasted_iota(jnp.int32, (CHUNK, BLK), 1)

    def products(p, grad):
        i, j = decode(pair_list, p)
        right = down[i]
        grad[0:used, :] = dot(turned[j, 0:used, :], jnp.concatenate([right, right], axis=0))

    def apply(p, grad):
        i, j = decode(pair_list, p)
        marks = [lane == 3 * j + c for c in range(3)]
        sums = [jnp.zeros((CHUNK, BLK), f32) for _ in range(3)]
        for r in range(used // CHUNK):
            place = slice(r * CHUNK, (r + 1) * CHUNK)
            parts, squared, remain = separation(rows, columns, penalty, i, j, place)
            decays = [jnp.exp2(squared * rates[k]) for k in range(RAD)]
            plain = None
            scaled = None
            for k in range(RAD):
                term = decays[k] * grad[place, k * BLK : (k + 1) * BLK]
                plain = term if plain is None else plain + term
                term = term * doubled[k]
                scaled = term if scaled is None else scaled + term
            weighted = remain * (plain + remain * scaled)
            pulls = [weighted * part for part in parts]
            sums = [s + pull for s, pull in zip(sums, pulls)]
            totals = [jnp.sum(pull, axis=1, keepdims=True) for pull in pulls]
            placed = jnp.where(
                marks[0],
                totals[0],
                jnp.where(marks[1], totals[1], jnp.where(marks[2], totals[2], 0.0)),
            )
            column_sum[place, :] += placed
        for c in range(3):
            row_sum[i, c] += sums[c]

    pairs_each = GROUP // 2
    first, second = grads[:pairs_each], grads[pairs_each:]

    @pl.when(count > 0)
    def _():
        for u, grad in enumerate(first):
            products(u, grad)

    def step(t, carry):
        base = GROUP * t
        for u, grad in enumerate(second):
            products(base + pairs_each + u, grad)
        for u, grad in enumerate(first):
            apply(base + u, grad)
        for u, grad in enumerate(first):
            products(base + GROUP + u, grad)
        for u, grad in enumerate(second):
            apply(base + pairs_each + u, grad)
        return carry

    lax.fori_loop(0, (count + GROUP - 1) // GROUP, step, 0)


def own_message_kernel(
    features,
    small,
    pairs,
    npairs,
    radial_width,
    weight,
    out_weight,
    message,
    own_list,
    ghost_list,
    tallies,
    rows,
    columns,
    penalty,
    turned,
    out_column,
    tables,
    *amps,
):
    split_lists(pairs, npairs, own_list, ghost_list, tallies)
    for b in range(CELLS):
        for c in range(3):
            n = CELLS * c + b
            rows[b, c : c + 1, :] = small[n : n + 1, :] * (1.0 / CUTOFF)
        rows[b, 3:8, :] = jnp.zeros((5, BLK), f32)
    masked = features[...] * occupancy(small)
    fill_tables(masked, jnp.concatenate([weight[...], weight[...]], axis=1), tables, 0)
    fill_transposed(masked, turned, 0)
    fill_columns(small, 0.0, columns, 0)
    fill_penalty(penalty)
    out_column[...] = jnp.broadcast_to(as_column(out_weight[...].astype(f32)), (F, BLK))
    message[...] = jnp.zeros(message.shape, f32)
    rates = decay_rates(inverse_widths(radial_width))
    message_pass(own_list, tallies[0], rows, columns, penalty, rates, tables, amps, message)


def as_column(row):
    size = (row.shape[1], row.shape[1])
    diagonal = lax.broadcasted_iota(jnp.int32, size, 0) == lax.broadcasted_iota(jnp.int32, size, 1)
    return jnp.sum(jnp.where(diagonal, row, 0.0), axis=1, keepdims=True)


def node_backward(
    message, masked, occupied, weight, update_weight, mix_weight, out_column, down
):
    whole = jnp.concatenate([message[b] for b in range(CELLS)], axis=1)
    scaled = (whole * MESSAGE_SCALE).astype(bf16)
    first_pre = dot(update_weight[...], scaled)
    first_gate = jax.nn.sigmoid(first_pre)
    updated = (masked + first_pre * first_gate).astype(bf16)
    second_pre = dot(mix_weight[...], updated)
    second_gate = jax.nn.sigmoid(second_pre)
    second_grad = (
        jnp.concatenate([out_column[...]] * CELLS, axis=1)
        * second_gate
        * (1.0 + second_pre * (1.0 - second_gate))
        * occupied
    ).astype(bf16)
    update_grad = dot(mix_weight[...], second_grad, ((0,), (0,)))
    first_grad = (update_grad * first_gate * (1.0 + first_pre * (1.0 - first_gate))).astype(bf16)
    downstream = (MESSAGE_SCALE * dot(update_weight[...], first_grad, ((0,), (0,)))).astype(bf16)
    for k in range(RAD):
        mixed = dot(weight[k * F : (k + 1) * F, :], downstream, ((0,), (0,)))
        mixed = (mixed * (4.0 * CUTOFF / CUTOFF_SQUARE)).astype(bf16)
        for b in range(CELLS):
            down[b, :, k * BLK : (k + 1) * BLK] = block_lanes(mixed, b)
    down[CELLS] = jnp.zeros((F, RAD * BLK), bf16)


def doubled_rates(inverse):
    return [value * (0.5 * CUTOFF_SQUARE) for value in inverse]


def collect_rows(row_sum, out, start=None):
    for b in range(CELLS):
        for c in range(3):
            total = jnp.sum(row_sum[b, c], axis=0, keepdims=True)
            n = CELLS * c + b
            m = 3 * b + c
            out[n : n + 1, :] = total if start is None else total - start[m : m + 1, :]


def ghost_kernel(
    features,
    small,
    below,
    above,
    small_below,
    small_above,
    own_message,
    rows,
    ghost_list,
    tallies,
    radial_width,
    weight,
    update_weight,
    mix_weight,
    out_column,
    row_force,
    ghost_below,
    ghost_above,
    down,
    message,
    tables,
    turned,
    columns,
    chosen,
    places,
    row_sum,
    column_sum,
    *buffers,
):
    amps, grads = buffers[:BATCH], buffers[BATCH:]
    doubled_weight = jnp.concatenate([weight[...], weight[...]], axis=1)
    smalls = (small_below, small_above)
    slots, most = near_first(smalls, (-CELL_SIDE, CELL_SIDE), small, places)
    fill_ghosts(
        smalls, (below, above), slots, places, doubled_weight, chosen, tables, turned, columns
    )
    message[...] = own_message[...]
    inverse = inverse_widths(radial_width)
    rates = decay_rates(inverse)
    count = tallies[1]
    for amp in amps:
        amp[...] = jnp.zeros(amp.shape, bf16)
    few = most <= FEWER

    def messages(used):
        message_pass(ghost_list, count, rows, columns, None, rates, tables, amps, message, used)

    pl.when(few)(partial(messages, FEWER))
    pl.when(jnp.logical_not(few))(partial(messages, BLK))
    occupied = occupancy(small)
    node_backward(
        message,
        features[...] * occupied,
        occupied,
        weight,
        update_weight,
        mix_weight,
        out_column,
        down,
    )
    row_sum[...] = jnp.zeros(row_sum.shape, f32)
    column_sum[...] = jnp.zeros(column_sum.shape, f32)

    def pulls(used):
        force_pass(
            ghost_list,
            count,
            rows,
            columns,
            None,
            rates,
            doubled_rates(inverse),
            turned,
            down,
            grads,
            row_sum,
            column_sum,
            used,
        )

    pl.when(few)(partial(pulls, FEWER))
    pl.when(jnp.logical_not(few))(partial(pulls, BLK))
    collect_rows(row_sum, row_force)
    return_ghosts(column_sum, chosen, (ghost_below, ghost_above))


def own_force_kernel(
    rows,
    columns,
    penalty,
    turned,
    row_force,
    down,
    own_list,
    tallies,
    radial_width,
    force,
    row_sum,
    column_sum,
    *grads,
):
    row_sum[...] = jnp.zeros(row_sum.shape, f32)
    column_sum[...] = jnp.zeros(column_sum.shape, f32)
    inverse = inverse_widths(radial_width)
    rates = decay_rates(inverse)
    force_pass(
        own_list,
        tallies[0],
        rows,
        columns,
        penalty,
        rates,
        doubled_rates(inverse),
        turned,
        down,
        grads,
        row_sum,
        column_sum,
    )
    collect_rows(row_sum, force, column_sum[...].T)
    force[...] += row_force[...]


def by_component(flat):
    return jnp.concatenate(
        [flat[3 * b + c : 3 * b + c + 1, :] for c in range(3) for b in range(CELLS)], axis=0
    )


def finish_kernel(
    force,
    from_above,
    from_below,
    small,
    momenta,
    masses,
    before,
    after,
    leaving,
    forces,
    positions_new,
    momenta_new,
    upward,
    downward,
    packet,
):
    physical = force[...] - by_component(from_above[...] + from_below[...])
    mass = jnp.concatenate([masses[...]] * 3, axis=0)
    current = small[0:PLACES, :]
    spring = -SPRING_RATE * mass * (2.0 * current - before[...] - after[...])
    total = physical + spring
    moved = momenta[...] + total
    placed = current + moved / mass
    forces[...] = total
    momenta_new[...] = moved
    positions_new[...] = placed
    packet[0:24, :] = placed
    packet[24:48, :] = moved
    packet[48:64, :] = jnp.zeros((16, BLK), f32)
    movers = jnp.concatenate([leaving[1:2, :], leaving[0:1, :]], axis=1)
    slot = lax.broadcasted_iota(jnp.int32, (ATOMS_DEV, 2 * MIG), 0)
    chosen = (slot == movers).astype(f32).astype(bf16)
    values = jnp.concatenate([packet[pl.ds(b, 8, stride=CELLS), :] for b in range(CELLS)], axis=1)
    high = values.astype(bf16)
    middle, low = halves(values - high.astype(f32))
    picked = dot(high, chosen) + (dot(middle, chosen) + dot(low, chosen))
    lane = lax.broadcasted_iota(jnp.int32, (8, 2 * MIG), 1)
    row = lax.broadcasted_iota(jnp.int32, (8, 2 * MIG), 0)
    shift = jnp.where(lane < MIG, -CELL_SIDE, CELL_SIDE)
    shifted = jnp.where(movers >= 0, picked + jnp.where(row == 2, shift, 0.0), 0.0)
    up = jnp.where(lane < MIG, shifted, 0.0)
    down = jnp.where(lane < MIG, 0.0, shifted)
    for q in range(6):
        upward[q] = up[q : q + 1, :]
        downward[q] = down[q : q + 1, :]


def effort(microseconds):
    return pl.CostEstimate(
        flops=int(microseconds * 1.0e9),
        transcendentals=0,
        bytes_accessed=int(microseconds * 3.0e6),
    )


def shape(dims, kind=f32):
    return jax.ShapeDtypeStruct(dims, kind)


def body(
    positions,
    momenta,
    features,
    masses,
    radial_width,
    msg_weight,
    update_weight,
    mix_weight,
    out_weight,
    counts,
    pairs,
    npairs,
    leaving,
):
    def ring(axis, step):
        count = lax.axis_size(axis)
        return [(i, (i + step) % count) for i in range(count)]

    up = ring("dom", 1)
    down_ring = ring("dom", -1)
    below = lax.ppermute(features, "dom", up)
    above = lax.ppermute(features, "dom", down_ring)
    weight = msg_weight.reshape(RAD * F, F)
    current = positions.reshape(PLACES, BLK)
    small = pl.pallas_call(
        pack_kernel,
        out_shape=shape((SMALL, BLK)),
        in_specs=[VMEM, SMEM],
        out_specs=VMEM,
        compiler_params=PARAMS,
        cost_estimate=effort(5),
    )(current, counts)
    small_below = lax.ppermute(small, "dom", up)
    small_above = lax.ppermute(small, "dom", down_ring)

    amp = pltpu.VMEM((RAD * BLK, BLK), bf16)
    grad = pltpu.VMEM((BLK, RAD * BLK), f32)
    row_sum = pltpu.VMEM((CELLS + 1, 3, CHUNK, BLK), f32)
    column_sum = pltpu.VMEM((BLK, BLK), f32)
    listed = shape((pairs.shape[1] + 2 * BATCH,), jnp.int32)

    def tables(blocks):
        return pltpu.VMEM((blocks, F, RAD * BLK), bf16)

    (
        own_message,
        own_list,
        ghost_list,
        tallies,
        rows,
        columns,
        penalty,
        turned,
        out_column,
    ) = pl.pallas_call(
        own_message_kernel,
        out_shape=(
            shape((CELLS + 1, F, BLK)),
            listed,
            listed,
            shape((2,), jnp.int32),
            shape((CELLS, 8, BLK)),
            shape((CELLS, 3, BLK, BLK)),
            shape((2, BLK, BLK)),
            shape((CELLS, BLK, BLK), bf16),
            shape((F, BLK)),
        ),
        in_specs=[VMEM] * 2 + [SMEM] * 3 + [VMEM] * 2,
        out_specs=(VMEM, SMEM, SMEM, SMEM) + (VMEM,) * 5,
        scratch_shapes=[tables(CELLS)] + [amp] * BATCH,
        compiler_params=PARAMS,
    )(
        features,
        small,
        pairs,
        npairs,
        radial_width,
        weight,
        out_weight.reshape(1, F),
    )
    late, own_message = lax.optimization_barrier((current, own_message))
    before = lax.ppermute(late, "bead", ring("bead", 1))
    after = lax.ppermute(late, "bead", ring("bead", -1))
    row_force, ghost_below, ghost_above, down = pl.pallas_call(
        ghost_kernel,
        out_shape=(
            shape((PLACES, BLK)),
            shape((PLACES, BLK)),
            shape((PLACES, BLK)),
            shape((CELLS + 1, F, RAD * BLK), bf16),
        ),
        in_specs=[VMEM] * 8 + [SMEM] * 3 + [VMEM] * 4,
        out_specs=(VMEM,) * 4,
        scratch_shapes=[
            pltpu.VMEM((CELLS + 1, F, BLK), f32),
            tables(2 * CELLS),
            pltpu.VMEM((2 * CELLS, BLK, BLK), bf16),
            pltpu.VMEM((2 * CELLS, 3, BLK, BLK), f32),
            pltpu.VMEM((2 * CELLS, BLK, BLK), bf16),
            pltpu.VMEM((BLK, BLK), f32),
            row_sum,
            column_sum,
        ]
        + [amp] * BATCH
        + [grad] * GROUP,
        compiler_params=PARAMS,
    )(
        features,
        small,
        below,
        above,
        small_below,
        small_above,
        own_message,
        rows,
        ghost_list,
        tallies,
        radial_width,
        weight,
        update_weight,
        mix_weight,
        out_column,
    )
    from_above = lax.ppermute(ghost_below, "dom", down_ring)
    from_below = lax.ppermute(ghost_above, "dom", up)
    force = pl.pallas_call(
        own_force_kernel,
        out_shape=shape((PLACES, BLK)),
        in_specs=[VMEM] * 6 + [SMEM] * 3,
        out_specs=VMEM,
        scratch_shapes=[row_sum, column_sum] + [grad] * GROUP,
        compiler_params=PARAMS,
    )(rows, columns, penalty, turned, row_force, down, own_list, tallies, radial_width)
    whole = shape((PLACES, BLK))
    packet = shape((6, 1, 2 * MIG))
    forces, positions_new, momenta_new, upward, downward = pl.pallas_call(
        finish_kernel,
        out_shape=(whole, whole, whole, packet, packet),
        in_specs=[VMEM] * 9,
        out_specs=(VMEM,) * 5,
        scratch_shapes=[pltpu.VMEM((64, BLK), f32)],
        compiler_params=PARAMS,
    )(
        force,
        from_above,
        from_below,
        small,
        momenta.reshape(PLACES, BLK),
        masses.reshape(CELLS, BLK),
        before,
        after,
        leaving,
    )
    arrivals = lax.ppermute(upward, "dom", up) + lax.ppermute(downward, "dom", down_ring)
    result = tuple(x.reshape(1, 3, ATOMS_DEV) for x in (forces, positions_new, momenta_new))
    return result + (arrivals.reshape(1, 6, 2 * MIG),)


def solution(mesh):
    split = P("bead", None, "dom")
    in_specs = (
        split,
        split,
        P(None, "dom"),
        P("dom"),
        P(),
        P(),
        P(),
        P(),
        P(),
        P("dom"),
        P(None, "dom"),
        P("dom"),
        P(None, "dom"),
    )
    out_specs = (split, split, split, split)
    return jax.shard_map(body, mesh=mesh, in_specs=in_specs, out_specs=out_specs, check_vma=False)
```

```python
from functools import partial

import jax
import jax.numpy as jnp
from jax import lax
from jax.experimental import pallas as pl
from jax.experimental.pallas import tpu as pltpu
from jax.sharding import PartitionSpec as P

F = 64
RAD = 4
BLK = 128
MIG = 64
CELLS = 8
ATOMS_DEV = CELLS * BLK
PLACES = 3 * CELLS
SMALL = PLACES + CELLS

CUTOFF = 6.0
CUTOFF_SQUARE = CUTOFF * CUTOFF
CELL_SIDE = 10.0
MESSAGE_SCALE = 0.25
SPRING_RATE = 0.2
LOG2E = 1.4426950408889634
FAR = 1.0e9
REACH = 1.001
FEWER = 96
CHUNK = 16
GROUP = 8
BATCH = 8

f32 = jnp.float32
bf16 = jnp.bfloat16
VMEM = pl.BlockSpec(memory_space=pltpu.VMEM)
SMEM = pl.BlockSpec(memory_space=pltpu.SMEM)
PARAMS = pltpu.CompilerParams(vmem_limit_bytes=32 * 1024 * 1024)


def dot(a, b, dims=((1,), (0,))):
    return lax.dot_general(a, b, (dims, ((), ())), preferred_element_type=f32)


def halves(x):
    high = x.astype(bf16)
    return high, (x - high.astype(f32)).astype(bf16)


def block_lanes(x, b):
    return x[:, b * BLK : (b + 1) * BLK]


def pack_kernel(positions, counts, small):
    lane = lax.broadcasted_iota(jnp.int32, (1, BLK), 1)
    small[0:PLACES, :] = positions[...]
    for b in range(CELLS):
        small[PLACES + b : PLACES + b + 1, :] = (lane < counts[b]).astype(f32)


def occupancy(small):
    return jnp.concatenate([small[PLACES + b : PLACES + b + 1, :] for b in range(CELLS)], axis=1)


def split_lists(pairs, npairs, own_list, ghost_list, tallies):
    def step(p, carry):
        own, ghost = carry
        i = pairs[0, p]
        j = pairs[1, p]
        mine = jnp.logical_and(j >= CELLS, j < 2 * CELLS)
        shifted = jnp.where(mine, j - CELLS, jnp.where(j >= 2 * CELLS, j - CELLS, j))
        code = i * 16 + shifted
        own_list[own] = code
        ghost_list[ghost] = code
        taken = mine.astype(jnp.int32)
        return own + taken, ghost + 1 - taken

    own, ghost = lax.fori_loop(0, npairs[0], step, (jnp.int32(0), jnp.int32(0)))
    for extra in range(2 * BATCH):
        own_list[own + extra] = CELLS * 16
        ghost_list[ghost + extra] = CELLS * 16
    tallies[0] = own
    tallies[1] = ghost


def fill_tables(masked, weight, tables, base):
    high, low = halves(masked)
    result = dot(weight, jnp.concatenate([high, low], axis=0))
    for b in range(CELLS):
        for k in range(RAD):
            tables[base + b, :, k * BLK : (k + 1) * BLK] = block_lanes(
                result[k * F : (k + 1) * F], b
            ).astype(bf16)


def fill_transposed(masked, turned, base):
    high = masked.astype(bf16).astype(f32)
    stacked = jnp.concatenate([high, masked - high], axis=0)
    for b in range(CELLS):
        turned[base + b] = block_lanes(stacked, b).T.astype(bf16)


def fill_columns(small, shift, columns, base):
    third = lax.broadcasted_iota(jnp.int32, (PLACES, BLK), 0) >= 2 * CELLS
    places = (small[0:PLACES, :] + jnp.where(third, shift, 0.0)) * (1.0 / CUTOFF)
    for b in range(CELLS):
        for c in range(3):
            n = CELLS * c + b
            columns[base + b, c] = jnp.broadcast_to(places[n : n + 1, :], (BLK, BLK)).T


def near_first(smalls, shifts, small, places):
    pieces = []
    for part, shift in zip(smalls, shifts):
        third = lax.broadcasted_iota(jnp.int32, (PLACES, BLK), 0) >= 2 * CELLS
        moved = (part[0:PLACES, :] + jnp.where(third, shift, 0.0)) * (1.0 / CUTOFF)
        pieces += [moved, part[PLACES:SMALL, :]]
    pieces.append(jnp.zeros((BLK - 2 * SMALL, BLK), f32))
    flat = jnp.concatenate(pieces, axis=0)
    places[...] = flat
    turned = flat.T
    heights = small[2 * CELLS : PLACES, :] * (1.0 / CUTOFF)
    held = small[PLACES:SMALL, :] > 0.5
    lowest = jnp.min(jnp.where(held, heights, FAR))
    highest = jnp.max(jnp.where(held, heights, -FAR))
    inside = jnp.logical_and(turned > lowest - REACH, turned < highest + REACH)
    present = pltpu.roll(turned, BLK - CELLS, 1) > 0.5
    near = jnp.where(jnp.logical_and(inside, present), 1.0, 0.0)
    ahead = lax.broadcasted_iota(jnp.int32, (BLK, BLK), 1) < lax.broadcasted_iota(
        jnp.int32, (BLK, BLK), 0
    )
    rank = dot(jnp.where(ahead, 1.0, 0.0).astype(bf16), near.astype(bf16))
    lane = lax.broadcasted_iota(jnp.int32, (1, BLK), 1)
    height_lane = jnp.bitwise_and(lax.shift_right_logical(lane, 3), 3) == 2
    height_lane = jnp.logical_and(height_lane, lane < 2 * SMALL)
    total = jnp.sum(near, axis=0, keepdims=True)
    most = jnp.max(jnp.where(height_lane, total, 0.0))
    return jnp.where(near > 0.5, rank, -1.0), most


def fill_ghosts(smalls, features, slots, places, weight, chosen, tables, turned, columns):
    lane = lax.broadcasted_iota(jnp.int32, (BLK, BLK), 1).astype(f32)
    for side in range(2):
        masked = features[side][...] * occupancy(smalls[side])
        high = masked.astype(bf16).astype(f32)
        low = masked - high
        for b in range(CELLS):
            n = side * CELLS + b
            place = side * SMALL + 2 * CELLS + b
            slot = jnp.broadcast_to(slots[:, place : place + 1], (BLK, BLK))
            pick = jnp.where(slot == lane, 1.0, 0.0).astype(bf16)
            chosen[n] = pick
            three = [
                places[side * SMALL + CELLS * c + b : side * SMALL + CELLS * c + b + 1, :]
                for c in range(3)
            ]
            here = jnp.concatenate(three + [jnp.zeros((5, BLK), f32)], axis=0)
            first = here.astype(bf16).astype(f32)
            second = (here - first).astype(bf16).astype(f32)
            parts = [block_lanes(high, b), block_lanes(low, b)]
            parts += [first, second, here - first - second]
            moved = dot(jnp.concatenate(parts, axis=0).astype(bf16), pick)
            spots = moved[2 * F : 2 * F + 8] + moved[2 * F + 8 : 2 * F + 16] + moved[2 * F + 16 :]
            for c in range(3):
                columns[n, c] = jnp.broadcast_to(spots[c : c + 1, :], (BLK, BLK)).T
            halved = moved[0 : 2 * F]
            result = dot(weight, halved.astype(bf16))
            for k in range(RAD):
                tables[n, :, k * BLK : (k + 1) * BLK] = result[k * F : (k + 1) * F].astype(bf16)
            turned[n] = halved.T.astype(bf16)


def return_ghosts(column_sum, chosen, outs):
    flat = column_sum[...].T
    for side in range(2):
        for b in range(CELLS):
            n = side * CELLS + b
            piece = jnp.concatenate([flat[3 * n : 3 * n + 3], jnp.zeros((5, BLK), f32)], axis=0)
            first = piece.astype(bf16).astype(f32)
            both = jnp.concatenate([first, piece - first], axis=0).astype(bf16)
            back = dot(both, chosen[n], ((1,), (1,)))
            outs[side][3 * b : 3 * b + 3, :] = back[0:3] + back[8:11]


def fill_penalty(penalty):
    same = lax.broadcasted_iota(jnp.int32, (BLK, BLK), 0) == lax.broadcasted_iota(
        jnp.int32, (BLK, BLK), 1
    )
    penalty[0] = jnp.zeros((BLK, BLK), f32)
    penalty[1] = jnp.where(same, FAR, 0.0)


def inverse_widths(radial_width):
    return [1.0 / (radial_width[k] * radial_width[k]) for k in range(RAD)]


def decay_rates(inverse):
    return [value * (-LOG2E * CUTOFF_SQUARE) for value in inverse]


def decode(pair_list, p):
    code = pair_list[p]
    return lax.shift_right_logical(code, 4), lax.bitwise_and(code, 15)


def separation(rows, columns, penalty, i, j, place):
    parts = [rows[i & 7, c : c + 1, :] - columns[j, c, place, :] for c in range(3)]
    squared = parts[0] * parts[0] + parts[1] * parts[1] + parts[2] * parts[2]
    if penalty is not None:
        squared = squared + penalty[(i == j).astype(jnp.int32), place, :]
    remain = jnp.maximum(1.0 - squared, 0.0)
    return parts, squared, remain


def message_pass(
    pair_list, count, rows, columns, penalty, rates, tables, amps, message, used=BLK
):
    def amplitudes(p, amp):
        i, j = decode(pair_list, p)
        for r in range(used // CHUNK):
            place = slice(r * CHUNK, (r + 1) * CHUNK)
            _, squared, remain = separation(rows, columns, penalty, i, j, place)
            cutoff = remain * remain
            for k in range(RAD):
                decay = jnp.exp2(squared * rates[k])
                value = decay * cutoff
                amp[k * BLK + r * CHUNK : k * BLK + (r + 1) * CHUNK, :] = value.astype(bf16)

    def multiply(p, amp):
        i, j = decode(pair_list, p)
        message[i] += dot(tables[j], amp[...])

    @pl.when(count > 0)
    def _():
        for u, amp in enumerate(amps):
            amplitudes(u, amp)

    def step(t, carry):
        for u, amp in enumerate(amps):
            multiply(BATCH * t + u, amp)
        for u, amp in enumerate(amps):
            amplitudes(BATCH * t + BATCH + u, amp)
        return carry

    groups = (count + BATCH - 1) // BATCH
    lax.fori_loop(0, groups - 1, step, 0)

    @pl.when(count > 0)
    def _():
        for u, amp in enumerate(amps):
            multiply(BATCH * (groups - 1) + u, amp)


def force_pass(
    pair_list, count, rows, columns, penalty, rates, doubled, turned, down, grads, row_sum, column_sum,
    used=BLK,
):
    lane = lax.broadcasted_iota(jnp.int32, (CHUNK, BLK), 1)

    def products(p, grad):
        i, j = decode(pair_list, p)
        right = down[i]
        grad[0:used, :] = dot(turned[j, 0:used, :], jnp.concatenate([right, right], axis=0))

    def apply(p, grad):
        i, j = decode(pair_list, p)
        marks = [lane == 3 * j + c for c in range(3)]
        sums = [jnp.zeros((CHUNK, BLK), f32) for _ in range(3)]
        for r in range(used // CHUNK):
            place = slice(r * CHUNK, (r + 1) * CHUNK)
            parts, squared, remain = separation(rows, columns, penalty, i, j, place)
            decays = [jnp.exp2(squared * rates[k]) for k in range(RAD)]
            plain = None
            scaled = None
            for k in range(RAD):
                term = decays[k] * grad[place, k * BLK : (k + 1) * BLK]
                plain = term if plain is None else plain + term
                term = term * doubled[k]
                scaled = term if scaled is None else scaled + term
            weighted = remain * (plain + remain * scaled)
            pulls = [weighted * part for part in parts]
            sums = [s + pull for s, pull in zip(sums, pulls)]
            totals = [jnp.sum(pull, axis=1, keepdims=True) for pull in pulls]
            placed = jnp.where(
                marks[0],
                totals[0],
                jnp.where(marks[1], totals[1], jnp.where(marks[2], totals[2], 0.0)),
            )
            column_sum[place, :] += placed
        for c in range(3):
            row_sum[i, c] += sums[c]

    pairs_each = GROUP // 2
    first, second = grads[:pairs_each], grads[pairs_each:]

    @pl.when(count > 0)
    def _():
        for u, grad in enumerate(first):
            products(u, grad)

    def step(t, carry):
        base = GROUP * t
        for u, grad in enumerate(second):
            products(base + pairs_each + u, grad)
        for u, grad in enumerate(first):
            apply(base + u, grad)
        for u, grad in enumerate(first):
            products(base + GROUP + u, grad)
        for u, grad in enumerate(second):
            apply(base + pairs_each + u, grad)
        return carry

    lax.fori_loop(0, (count + GROUP - 1) // GROUP, step, 0)


def own_message_kernel(
    features,
    small,
    pairs,
    npairs,
    radial_width,
    weight,
    out_weight,
    message,
    own_list,
    ghost_list,
    tallies,
    rows,
    columns,
    turned,
    out_column,
    tables,
    penalty,
    *amps,
):
    split_lists(pairs, npairs, own_list, ghost_list, tallies)
    for b in range(CELLS):
        for c in range(3):
            n = CELLS * c + b
            rows[b, c : c + 1, :] = small[n : n + 1, :] * (1.0 / CUTOFF)
        rows[b, 3:8, :] = jnp.zeros((5, BLK), f32)
    masked = features[...] * occupancy(small)
    fill_tables(masked, jnp.concatenate([weight[...], weight[...]], axis=1), tables, 0)
    fill_transposed(masked, turned, 0)
    fill_columns(small, 0.0, columns, 0)
    fill_penalty(penalty)
    out_column[...] = jnp.broadcast_to(as_column(out_weight[...].astype(f32)), (F, BLK))
    message[...] = jnp.zeros(message.shape, f32)
    rates = decay_rates(inverse_widths(radial_width))
    message_pass(own_list, tallies[0], rows, columns, penalty, rates, tables, amps, message)


def as_column(row):
    size = (row.shape[1], row.shape[1])
    diagonal = lax.broadcasted_iota(jnp.int32, size, 0) == lax.broadcasted_iota(jnp.int32, size, 1)
    return jnp.sum(jnp.where(diagonal, row, 0.0), axis=1, keepdims=True)


def node_backward(
    message, masked, occupied, weight, update_weight, mix_weight, out_column, down
):
    whole = jnp.concatenate([message[b] for b in range(CELLS)], axis=1)
    scaled = (whole * MESSAGE_SCALE).astype(bf16)
    first_pre = dot(update_weight[...], scaled)
    first_gate = jax.nn.sigmoid(first_pre)
    updated = (masked + first_pre * first_gate).astype(bf16)
    second_pre = dot(mix_weight[...], updated)
    second_gate = jax.nn.sigmoid(second_pre)
    second_grad = (
        jnp.concatenate([out_column[...]] * CELLS, axis=1)
        * second_gate
        * (1.0 + second_pre * (1.0 - second_gate))
        * occupied
    ).astype(bf16)
    update_grad = dot(mix_weight[...], second_grad, ((0,), (0,)))
    first_grad = (update_grad * first_gate * (1.0 + first_pre * (1.0 - first_gate))).astype(bf16)
    downstream = (MESSAGE_SCALE * dot(update_weight[...], first_grad, ((0,), (0,)))).astype(bf16)
    for k in range(RAD):
        mixed = dot(weight[k * F : (k + 1) * F, :], downstream, ((0,), (0,)))
        mixed = (mixed * (4.0 * CUTOFF / CUTOFF_SQUARE)).astype(bf16)
        for b in range(CELLS):
            down[b, :, k * BLK : (k + 1) * BLK] = block_lanes(mixed, b)
    down[CELLS] = jnp.zeros((F, RAD * BLK), bf16)


def doubled_rates(inverse):
    return [value * (0.5 * CUTOFF_SQUARE) for value in inverse]


def collect_rows(row_sum, out, start=None):
    for b in range(CELLS):
        for c in range(3):
            total = jnp.sum(row_sum[b, c], axis=0, keepdims=True)
            n = CELLS * c + b
            m = 3 * b + c
            out[n : n + 1, :] = total if start is None else total - start[m : m + 1, :]


def ghost_kernel(
    features,
    small,
    below,
    above,
    small_below,
    small_above,
    own_message,
    rows,
    ghost_list,
    tallies,
    radial_width,
    weight,
    update_weight,
    mix_weight,
    out_column,
    row_force,
    ghost_below,
    ghost_above,
    down,
    message,
    tables,
    turned,
    columns,
    chosen,
    places,
    row_sum,
    column_sum,
    *buffers,
):
    amps, grads = buffers[:BATCH], buffers[BATCH:]
    doubled_weight = jnp.concatenate([weight[...], weight[...]], axis=1)
    smalls = (small_below, small_above)
    slots, most = near_first(smalls, (-CELL_SIDE, CELL_SIDE), small, places)
    fill_ghosts(
        smalls, (below, above), slots, places, doubled_weight, chosen, tables, turned, columns
    )
    message[...] = own_message[...]
    inverse = inverse_widths(radial_width)
    rates = decay_rates(inverse)
    count = tallies[1]
    for amp in amps:
        amp[...] = jnp.zeros(amp.shape, bf16)
    few = most <= FEWER

    def messages(used):
        message_pass(ghost_list, count, rows, columns, None, rates, tables, amps, message, used)

    pl.when(few)(partial(messages, FEWER))
    pl.when(jnp.logical_not(few))(partial(messages, BLK))
    occupied = occupancy(small)
    node_backward(
        message,
        features[...] * occupied,
        occupied,
        weight,
        update_weight,
        mix_weight,
        out_column,
        down,
    )
    row_sum[...] = jnp.zeros(row_sum.shape, f32)
    column_sum[...] = jnp.zeros(column_sum.shape, f32)

    def pulls(used):
        force_pass(
            ghost_list,
            count,
            rows,
            columns,
            None,
            rates,
            doubled_rates(inverse),
            turned,
            down,
            grads,
            row_sum,
            column_sum,
            used,
        )

    pl.when(few)(partial(pulls, FEWER))
    pl.when(jnp.logical_not(few))(partial(pulls, BLK))
    collect_rows(row_sum, row_force)
    return_ghosts(column_sum, chosen, (ghost_below, ghost_above))


def own_force_kernel(
    rows,
    columns,
    turned,
    row_force,
    down,
    own_list,
    tallies,
    radial_width,
    force,
    row_sum,
    column_sum,
    *grads,
):
    row_sum[...] = jnp.zeros(row_sum.shape, f32)
    column_sum[...] = jnp.zeros(column_sum.shape, f32)
    inverse = inverse_widths(radial_width)
    rates = decay_rates(inverse)
    force_pass(
        own_list,
        tallies[0],
        rows,
        columns,
        None,
        rates,
        doubled_rates(inverse),
        turned,
        down,
        grads,
        row_sum,
        column_sum,
    )
    collect_rows(row_sum, force, column_sum[...].T)
    force[...] += row_force[...]


def by_component(flat):
    return jnp.concatenate(
        [flat[3 * b + c : 3 * b + c + 1, :] for c in range(3) for b in range(CELLS)], axis=0
    )


def finish_kernel(
    force,
    from_above,
    from_below,
    small,
    momenta,
    masses,
    before,
    after,
    leaving,
    forces,
    positions_new,
    momenta_new,
    upward,
    downward,
    packet,
):
    physical = force[...] - by_component(from_above[...] + from_below[...])
    mass = jnp.concatenate([masses[...]] * 3, axis=0)
    current = small[0:PLACES, :]
    spring = -SPRING_RATE * mass * (2.0 * current - before[...] - after[...])
    total = physical + spring
    moved = momenta[...] + total
    placed = current + moved / mass
    forces[...] = total
    momenta_new[...] = moved
    positions_new[...] = placed
    packet[0:24, :] = placed
    packet[24:48, :] = moved
    packet[48:64, :] = jnp.zeros((16, BLK), f32)
    movers = jnp.concatenate([leaving[1:2, :], leaving[0:1, :]], axis=1)
    slot = lax.broadcasted_iota(jnp.int32, (ATOMS_DEV, 2 * MIG), 0)
    chosen = (slot == movers).astype(f32).astype(bf16)
    values = jnp.concatenate([packet[pl.ds(b, 8, stride=CELLS), :] for b in range(CELLS)], axis=1)
    high = values.astype(bf16)
    middle, low = halves(values - high.astype(f32))
    picked = dot(high, chosen) + (dot(middle, chosen) + dot(low, chosen))
    lane = lax.broadcasted_iota(jnp.int32, (8, 2 * MIG), 1)
    row = lax.broadcasted_iota(jnp.int32, (8, 2 * MIG), 0)
    shift = jnp.where(lane < MIG, -CELL_SIDE, CELL_SIDE)
    shifted = jnp.where(movers >= 0, picked + jnp.where(row == 2, shift, 0.0), 0.0)
    up = jnp.where(lane < MIG, shifted, 0.0)
    down = jnp.where(lane < MIG, 0.0, shifted)
    for q in range(6):
        upward[q] = up[q : q + 1, :]
        downward[q] = down[q : q + 1, :]


def effort(microseconds):
    return pl.CostEstimate(
        flops=int(microseconds * 1.0e9),
        transcendentals=0,
        bytes_accessed=int(microseconds * 3.0e6),
    )


def shape(dims, kind=f32):
    return jax.ShapeDtypeStruct(dims, kind)


def body(
    positions,
    momenta,
    features,
    masses,
    radial_width,
    msg_weight,
    update_weight,
    mix_weight,
    out_weight,
    counts,
    pairs,
    npairs,
    leaving,
):
    def ring(axis, step):
        count = lax.axis_size(axis)
        return [(i, (i + step) % count) for i in range(count)]

    up = ring("dom", 1)
    down_ring = ring("dom", -1)
    below = lax.ppermute(features, "dom", up)
    above = lax.ppermute(features, "dom", down_ring)
    weight = msg_weight.reshape(RAD * F, F)
    current = positions.reshape(PLACES, BLK)
    small = pl.pallas_call(
        pack_kernel,
        out_shape=shape((SMALL, BLK)),
        in_specs=[VMEM, SMEM],
        out_specs=VMEM,
        compiler_params=PARAMS,
        cost_estimate=effort(5),
    )(current, counts)
    small_below = lax.ppermute(small, "dom", up)
    small_above = lax.ppermute(small, "dom", down_ring)

    amp = pltpu.VMEM((RAD * BLK, BLK), bf16)
    grad = pltpu.VMEM((BLK, RAD * BLK), f32)
    row_sum = pltpu.VMEM((CELLS + 1, 3, CHUNK, BLK), f32)
    column_sum = pltpu.VMEM((BLK, BLK), f32)
    listed = shape((pairs.shape[1] + 2 * BATCH,), jnp.int32)

    def tables(blocks):
        return pltpu.VMEM((blocks, F, RAD * BLK), bf16)

    (
        own_message,
        own_list,
        ghost_list,
        tallies,
        rows,
        columns,
        turned,
        out_column,
    ) = pl.pallas_call(
        own_message_kernel,
        out_shape=(
            shape((CELLS + 1, F, BLK)),
            listed,
            listed,
            shape((2,), jnp.int32),
            shape((CELLS, 8, BLK)),
            shape((CELLS, 3, BLK, BLK)),
            shape((CELLS, BLK, BLK), bf16),
            shape((F, BLK)),
        ),
        in_specs=[VMEM] * 2 + [SMEM] * 3 + [VMEM] * 2,
        out_specs=(VMEM, SMEM, SMEM, SMEM) + (VMEM,) * 4,
        scratch_shapes=[tables(CELLS), pltpu.VMEM((2, BLK, BLK), f32)] + [amp] * BATCH,
        compiler_params=PARAMS,
    )(
        features,
        small,
        pairs,
        npairs,
        radial_width,
        weight,
        out_weight.reshape(1, F),
    )
    late, own_message = lax.optimization_barrier((current, own_message))
    before = lax.ppermute(late, "bead", ring("bead", 1))
    after = lax.ppermute(late, "bead", ring("bead", -1))
    row_force, ghost_below, ghost_above, down = pl.pallas_call(
        ghost_kernel,
        out_shape=(
            shape((PLACES, BLK)),
            shape((PLACES, BLK)),
            shape((PLACES, BLK)),
            shape((CELLS + 1, F, RAD * BLK), bf16),
        ),
        in_specs=[VMEM] * 8 + [SMEM] * 3 + [VMEM] * 4,
        out_specs=(VMEM,) * 4,
        scratch_shapes=[
            pltpu.VMEM((CELLS + 1, F, BLK), f32),
            tables(2 * CELLS),
            pltpu.VMEM((2 * CELLS, BLK, BLK), bf16),
            pltpu.VMEM((2 * CELLS, 3, BLK, BLK), f32),
            pltpu.VMEM((2 * CELLS, BLK, BLK), bf16),
            pltpu.VMEM((BLK, BLK), f32),
            row_sum,
            column_sum,
        ]
        + [amp] * BATCH
        + [grad] * GROUP,
        compiler_params=PARAMS,
    )(
        features,
        small,
        below,
        above,
        small_below,
        small_above,
        own_message,
        rows,
        ghost_list,
        tallies,
        radial_width,
        weight,
        update_weight,
        mix_weight,
        out_column,
    )
    from_above = lax.ppermute(ghost_below, "dom", down_ring)
    from_below = lax.ppermute(ghost_above, "dom", up)
    force = pl.pallas_call(
        own_force_kernel,
        out_shape=shape((PLACES, BLK)),
        in_specs=[VMEM] * 5 + [SMEM] * 3,
        out_specs=VMEM,
        scratch_shapes=[row_sum, column_sum] + [grad] * GROUP,
        compiler_params=PARAMS,
    )(rows, columns, turned, row_force, down, own_list, tallies, radial_width)
    whole = shape((PLACES, BLK))
    packet = shape((6, 1, 2 * MIG))
    forces, positions_new, momenta_new, upward, downward = pl.pallas_call(
        finish_kernel,
        out_shape=(whole, whole, whole, packet, packet),
        in_specs=[VMEM] * 9,
        out_specs=(VMEM,) * 5,
        scratch_shapes=[pltpu.VMEM((64, BLK), f32)],
        compiler_params=PARAMS,
    )(
        force,
        from_above,
        from_below,
        small,
        momenta.reshape(PLACES, BLK),
        masses.reshape(CELLS, BLK),
        before,
        after,
        leaving,
    )
    arrivals = lax.ppermute(upward, "dom", up) + lax.ppermute(downward, "dom", down_ring)
    result = tuple(x.reshape(1, 3, ATOMS_DEV) for x in (forces, positions_new, momenta_new))
    return result + (arrivals.reshape(1, 6, 2 * MIG),)


def solution(mesh):
    split = P("bead", None, "dom")
    in_specs = (
        split,
        split,
        P(None, "dom"),
        P("dom"),
        P(),
        P(),
        P(),
        P(),
        P(),
        P("dom"),
        P(None, "dom"),
        P("dom"),
        P(None, "dom"),
    )
    out_specs = (split, split, split, split)
    return jax.shard_map(body, mesh=mesh, in_specs=in_specs, out_specs=out_specs, check_vma=False)
```
